32 devices in a mesh: dp: 8 (over y, x, core), mp: 4 (over z).
Axes of the slice: x: 2, y: 2, z: 4, core: 2. Of those that a mesh axis runs over, the one named last changes fastest.
Arguments:
- tokens: bfloat16 [16384, 2048], P(('dp', 'mp')), may hold values from -6 to 6
- cotangent: bfloat16 [16384, 2048], P(('dp', 'mp'))
- lengths: int32 [8, 2], P('dp'), may hold values from 1 to 2047, as said below
- w_qkv: float32 [2048, 6144], P('dp', 'mp')
- w_out: float32 [2048, 2048], P('mp', 'dp')
- w_up: float32 [2048, 8192], P('dp', 'mp'), may hold values from -0.125 to 0.125
- w_down: float32 [8192, 2048], P('mp', 'dp')
- norm_vec: float32 [6, 2048], replicated
- b_qkv: float32 [6144], P('mp'), may hold values from -1.2 to 1.2
- b_up: float32 [8192], P('mp'), may hold values from -3 to 3
- m_qkv: float32 [2048, 6144], P('dp', 'mp')
- m_out: float32 [2048, 2048], P('mp', 'dp')
- m_up: float32 [2048, 8192], P('dp', 'mp')
- m_down: float32 [8192, 2048], P('mp', 'dp')
- m_norm: float32 [6, 2048], replicated
- m_bqkv: float32 [6144], P('mp')
- m_bup: float32 [8192], P('mp')
- v_qkv: float32 [2048, 6144], P('dp', 'mp'), as said below
- v_out: float32 [2048, 2048], P('mp', 'dp'), as said below
- v_up: float32 [2048, 8192], P('dp', 'mp'), as said below
- v_down: float32 [8192, 2048], P('mp', 'dp'), as said below
- v_norm: float32 [6, 2048], replicated, as said below
- v_bqkv: float32 [6144], P('mp'), as said below
- v_bup: float32 [8192], P('mp'), as said below
Outputs:
- layer_out: bfloat16 [16384, 2048], P(('dp', 'mp'))
- grad_in: bfloat16 [16384, 2048], P(('dp', 'mp'))
- grad_norm: float32 [], replicated
- upd_qkv: float32 [2048, 6144], P('dp', 'mp')
- upd_out: float32 [2048, 2048], P('mp', 'dp')
- upd_up: float32 [2048, 8192], P('dp', 'mp')
- upd_down: float32 [8192, 2048], P('mp', 'dp')
- upd_norm: float32 [6, 2048], replicated
- upd_bqkv: float32 [6144], P('mp')
- upd_bup: float32 [8192], P('mp')
- mom_qkv: float32 [2048, 6144], P('dp', 'mp')
- mom_out: float32 [2048, 2048], P('mp', 'dp')
- mom_up: float32 [2048, 8192], P('dp', 'mp')
- mom_down: float32 [8192, 2048], P('mp', 'dp')
- mom_norm: float32 [6, 2048], replicated
- mom_bqkv: float32 [6144], P('mp')
- mom_bup: float32 [8192], P('mp')
- sec_qkv: float32 [2048, 6144], P('dp', 'mp')
- sec_out: float32 [2048, 2048], P('mp', 'dp')
- sec_up: float32 [2048, 8192], P('dp', 'mp')
- sec_down: float32 [8192, 2048], P('mp', 'dp')
- sec_norm: float32 [6, 2048], replicated
- sec_bqkv: float32 [6144], P('mp')
- sec_bup: float32 [8192], P('mp')
The draws below stay inside these ranges and needn't reach their ends.
Inputs may be any that keep to these rules, and one draw needn't show every extreme that they name: lengths[g, 0] is at least 1537, lengths[g, 1] is at least 1, and their sum is at most 2048. `v_qkv`: every entry is positive. `v_out`: every entry is positive. `v_up`: every entry is positive. `v_down`: every entry is positive. `v_norm`: every entry is positive. `v_bqkv`: every entry is positive. `v_bup`: every entry is positive.
All inputs are finite; a program needn't handle non-finite values.
Results may differ from the reference program's by a relative error of at most 0.015.
The reference program's roundings to bfloat16 on the way count: a program that leaves them out, or rounds other values in their place, can miss the bound.
Values may be sent and summed in bfloat16 or wider, within the bound.
No kernel may reach another device: no remote copies, remote signals or barrier semaphores. Data moves between devices by JAX's collectives and lax.ppermute only.
A program may use at most 320 MiB of HBM per device.

```python
import math
import jax
import jax.numpy as jnp
from jax import lax

D = 2048
HEADS = 16
HD = 128
ROT = 32
FF = 8192
GROUP_TOK = 2048
STEP = 10
GROUPS = 8
TOK_DEV = 512
TOKENS = 16384


CLIP_NORM = 1.0


def rising(count, top):
    place = jnp.arange(count, dtype=jnp.float32) / max(count - 1, 1)
    return top ** (place - 0.5)


def grad_entry():
    return CLIP_NORM / math.sqrt(4 * D * D + 2 * D * FF + 3 * D + FF + 6 * D)


def head_rise():
    return jnp.repeat(rising(HEADS, 3.0), 3 * HD)


def first_state(key, size_map):
    return jax.random.normal(key, size_map.shape, jnp.float32) * (0.1 / 0.9) * size_map


def second_state(key, size_map):
    factor = jax.random.uniform(key, size_map.shape, jnp.float32, 1.0, 4.0)
    return factor * (0.05 / 0.95) * size_map * size_map


def size_qkv():
    return grad_entry() * 1.8 * rising(D, 3.0)[:, None] * head_rise()[None, :]


def size_out():
    return grad_entry() * 0.2 * jnp.ones((D, 1), jnp.float32) * rising(D, 3.0)[None, :]


def size_up():
    return grad_entry() * 0.12 * rising(D, 3.0)[:, None] * rising(FF, 3.0)[None, :]


def size_down():
    return grad_entry() * 0.5 * jnp.ones((FF, 1), jnp.float32) * rising(D, 3.0)[None, :]


def size_norm():
    rows = jnp.array([3.7, 3.7, 1.2, 1.2, 0.8, 0.8], jnp.float32)[:, None]
    return grad_entry() * rows * jnp.ones((1, D), jnp.float32)


def size_bqkv():
    return grad_entry() * 1.6 * head_rise()


def size_bup():
    return grad_entry() * 0.11 * rising(FF, 3.0)


def draw_lengths(key, part):
    key = jax.random.fold_in(key, 11)
    pad_key, second_key, pick_key = jax.random.split(key, 3)
    rows = jnp.arange(GROUPS, dtype=jnp.int32)
    chosen = jax.random.randint(pick_key, (), 0, GROUPS)
    pad_first = jax.random.randint(pad_key, (GROUPS,), 1, TOK_DEV)
    pad_first = jnp.where(rows == chosen, 1, pad_first)
    second_len = jax.random.randint(second_key, (GROUPS,), 1, pad_first + 1)
    second_len = jnp.where(rows == chosen, 1, second_len)
    first_len = GROUP_TOK - pad_first
    return jnp.stack([first_len, second_len], axis=-1).astype(jnp.int32)


def draw_cotangent(key, part):
    key = jax.random.fold_in(key, 5)
    base = jax.random.normal(key, (TOKENS, D), jnp.float32)
    return (base * rising(D, 3.0)[None, :]).astype(jnp.bfloat16)


def draw_w_qkv(key, part):
    key = jax.random.fold_in(key, 2)
    kind = jnp.arange(3 * D) // HD % 3
    scale = jnp.where(kind < 2, math.sqrt(2.0 / D), math.sqrt(1.0 / D)).astype(jnp.float32)
    return jax.random.normal(key, (D, 3 * D), jnp.float32) * scale[None, :]


def draw_w_out(key, part):
    key = jax.random.fold_in(key, 3)
    fan = max(D * 16 // GROUP_TOK, 1)
    return jax.random.normal(key, (D, D), jnp.float32) * fan ** (-0.5) * rising(D, 3.0)[:, None]


def draw_w_down(key, part):
    key = jax.random.fold_in(key, 4)
    return jax.random.normal(key, (FF, D), jnp.float32) * FF ** (-0.5) * rising(FF, 3.0)[:, None]


def draw_norm_vec(key, part):
    key = jax.random.fold_in(key, 7)
    gain_key, shift_key = jax.random.split(key)
    top = 3.0
    gains = rising(D, top)[None, :] * jax.random.uniform(gain_key, (2, D), jnp.float32, 0.85, 1.15)
    shifts = jax.random.normal(shift_key, (4, D), jnp.float32) * 0.5
    return jnp.stack([gains[0], shifts[0], gains[1], shifts[1], shifts[2], shifts[3]])


def draw_m_qkv(key, part):
    return first_state(jax.random.fold_in(key, 21), size_qkv())


def draw_m_out(key, part):
    return first_state(jax.random.fold_in(key, 22), size_out())


def draw_m_up(key, part):
    return first_state(jax.random.fold_in(key, 23), size_up())


def draw_m_down(key, part):
    return first_state(jax.random.fold_in(key, 24), size_down())


def draw_m_norm(key, part):
    return first_state(jax.random.fold_in(key, 25), size_norm())


def draw_m_bqkv(key, part):
    return first_state(jax.random.fold_in(key, 26), size_bqkv())


def draw_m_bup(key, part):
    return first_state(jax.random.fold_in(key, 27), size_bup())


def draw_v_qkv(key, part):
    return second_state(jax.random.fold_in(key, 31), size_qkv())


def draw_v_out(key, part):
    return second_state(jax.random.fold_in(key, 32), size_out())


def draw_v_up(key, part):
    return second_state(jax.random.fold_in(key, 33), size_up())


def draw_v_down(key, part):
    return second_state(jax.random.fold_in(key, 34), size_down())


def draw_v_norm(key, part):
    return second_state(jax.random.fold_in(key, 35), size_norm())


def draw_v_bqkv(key, part):
    return second_state(jax.random.fold_in(key, 36), size_bqkv())


def draw_v_bup(key, part):
    return second_state(jax.random.fold_in(key, 37), size_bup())


def steps_of(rng, extent, cuts, least, top_value):
    def one(axis_at, parts):
        draws = jax.random.uniform(jax.random.fold_in(jax.random.fold_in(rng, 6), axis_at), (parts,), jnp.float32, least / len(cuts), top_value / len(cuts))
        return jnp.repeat(jnp.exp(draws), extent[axis_at] // parts).reshape((-1,) + (1,) * (len(extent) - axis_at - 1))

    level = one(*cuts[0])
    for cut in cuts[1:]:
        level = level * one(*cut)
    return level


def normal_values(rng, extent, deviation, bound, cuts=(), kind=jnp.bfloat16):
    values = deviation * jax.random.normal(rng, extent, jnp.float32)
    if cuts:
        values = values * steps_of(rng, extent, cuts, -0.22, 0.18)
    return jnp.clip(values, -bound, bound).astype(kind)


def setup_inputs(seed: int = 0) -> dict:
    key_list = jax.random.split(jax.random.key(seed), 25)
    tokens = normal_values(key_list[0], (TOKENS, D), 1.0, 6.0, ((0, 32),))
    cotangent = draw_cotangent(jax.random.fold_in(key_list[24], 71), 0)
    lengths = draw_lengths(jax.random.fold_in(key_list[24], 71), 0)
    w_qkv = draw_w_qkv(jax.random.fold_in(key_list[24], 71), 0)
    w_out = draw_w_out(jax.random.fold_in(key_list[24], 71), 0)
    w_up = normal_values(key_list[5], (D, FF), D ** -0.5, 0.125, ((0, 8), (1, 4)), jnp.float32)
    w_down = draw_w_down(jax.random.fold_in(key_list[24], 71), 0)
    norm_vec = draw_norm_vec(jax.random.fold_in(key_list[24], 71), 0)
    b_qkv = normal_values(key_list[8], (3 * D,), 0.2, 1.2, ((0, 4),), jnp.float32)
    b_up = normal_values(key_list[9], (FF,), 0.5, 3.0, ((0, 4),), jnp.float32)
    m_qkv = draw_m_qkv(jax.random.fold_in(key_list[24], 71), 0)
    m_out = draw_m_out(jax.random.fold_in(key_list[24], 71), 0)
    m_up = draw_m_up(jax.random.fold_in(key_list[24], 71), 0)
    m_down = draw_m_down(jax.random.fold_in(key_list[24], 71), 0)
    m_norm = draw_m_norm(jax.random.fold_in(key_list[24], 71), 0)
    m_bqkv = draw_m_bqkv(jax.random.fold_in(key_list[24], 71), 0)
    m_bup = draw_m_bup(jax.random.fold_in(key_list[24], 71), 0)
    v_qkv = draw_v_qkv(jax.random.fold_in(key_list[24], 71), 0)
    v_out = draw_v_out(jax.random.fold_in(key_list[24], 71), 0)
    v_up = draw_v_up(jax.random.fold_in(key_list[24], 71), 0)
    v_down = draw_v_down(jax.random.fold_in(key_list[24], 71), 0)
    v_norm = draw_v_norm(jax.random.fold_in(key_list[24], 71), 0)
    v_bqkv = draw_v_bqkv(jax.random.fold_in(key_list[24], 71), 0)
    v_bup = draw_v_bup(jax.random.fold_in(key_list[24], 71), 0)
    return {"tokens": tokens, "cotangent": cotangent, "lengths": lengths, "w_qkv": w_qkv, "w_out": w_out, "w_up": w_up, "w_down": w_down, "norm_vec": norm_vec, "b_qkv": b_qkv, "b_up": b_up, "m_qkv": m_qkv, "m_out": m_out, "m_up": m_up, "m_down": m_down, "m_norm": m_norm, "m_bqkv": m_bqkv, "m_bup": m_bup, "v_qkv": v_qkv, "v_out": v_out, "v_up": v_up, "v_down": v_down, "v_norm": v_norm, "v_bqkv": v_bqkv, "v_bup": v_bup}


@jax.custom_vjp
def low(v):
    return lax.optimization_barrier(v.astype(jnp.bfloat16)).astype(jnp.float32)

@jax.custom_vjp
def low_back(v):
    return v

def low_keep(v):
    return (low(v), None)

def low_pass(kept, grad):
    return (grad,)

def back_keep(v):
    return (v, None)

def back_low(kept, grad):
    return (low(grad),)
low.defvjp(low_keep, low_pass)
low_back.defvjp(back_keep, back_low)
LN_EPS = 1e-05
ROPE_BASE = 10000.0
CLIP_NORM = 1.0
BETA_ONE = 0.9
BETA_TWO = 0.95
ADAM_EPS = 1e-08
DECAY = 0.01
RATE_SMALL = 1.0
HIGH = lax.Precision.HIGHEST

def layer_norm(values, gain, shift):
    centre = values - lax.optimization_barrier(jnp.mean(values, axis=-1, keepdims=True))
    spread = lax.optimization_barrier(jnp.mean(centre * centre, axis=-1, keepdims=True))
    return centre * lax.rsqrt(spread + LN_EPS) * gain + shift

def row_layout(lengths_row, count):
    first_len = lengths_row[0]
    used = lengths_row[0] + lengths_row[1]
    row_ids = jnp.arange(count, dtype=jnp.int32)
    segment = (row_ids >= first_len).astype(jnp.int32) + (row_ids >= used).astype(jnp.int32)
    begin = jnp.where(segment == 0, 0, jnp.where(segment == 1, first_len, used)).astype(jnp.int32)
    position = (row_ids - begin).astype(jnp.float32)
    return (segment, position, row_ids < used)

def rotary(values, position):
    half = ROT // 2
    inverse = ROPE_BASE ** (-jnp.arange(half, dtype=jnp.float32) * 2.0 / ROT)
    angle = position[:, None] * inverse[None, :]
    angle = jnp.concatenate([angle, angle], axis=-1)
    cosine = jnp.cos(angle)[:, None, :]
    sine = jnp.sin(angle)[:, None, :]
    turned = values[..., :ROT]
    rolled = jnp.concatenate([-turned[..., half:], turned[..., :half]], axis=-1)
    return jnp.concatenate([turned * cosine + rolled * sine, values[..., ROT:]], axis=-1)

def attend(query, keyset, valueset, segment):
    width = min(512, GROUP_TOK)
    blocks = GROUP_TOK // width
    row_ids = jnp.arange(GROUP_TOK, dtype=jnp.int32)

    def one_block(packed):
        query_block, rows_block, seg_block = packed
        raw = jnp.einsum('qhd,khd->hqk', query_block, keyset, precision=HIGH, preferred_element_type=jnp.float32) * HD ** (-0.5)
        raw = low_back(raw)
        allowed = (seg_block[:, None] == segment[None, :]) & (row_ids[None, :] <= rows_block[:, None])
        masked = jnp.where(allowed[None], raw, -jnp.inf)
        top = lax.optimization_barrier(jnp.max(masked, axis=-1, keepdims=True))
        expo = jnp.exp(masked - top)
        prob = expo / lax.optimization_barrier(jnp.sum(expo, axis=-1, keepdims=True))
        return jnp.einsum('hqk,khd->qhd', low(prob), valueset, precision=HIGH, preferred_element_type=jnp.float32)
    outs = lax.map(jax.checkpoint(one_block), (query.reshape(blocks, width, HEADS, HD), row_ids.reshape(blocks, width), segment.reshape(blocks, width)))
    return outs.reshape(GROUP_TOK, HEADS * HD)

def group_forward(rows_in, lengths_row, low_qkv, low_out, low_up, low_down, gains, bias_mix, bias_hidden):
    segment, position, live = row_layout(lengths_row, GROUP_TOK)
    first = low(layer_norm(rows_in, gains[0], gains[1]))
    second = low(layer_norm(rows_in, gains[2], gains[3]))
    mixed = jnp.dot(first, low_qkv, precision=HIGH, preferred_element_type=jnp.float32) + bias_mix
    mixed = low_back(mixed).reshape(GROUP_TOK, HEADS, 3, HD)
    query = low(rotary(mixed[:, :, 0], position))
    keyset = low(rotary(mixed[:, :, 1], position))
    valueset = low(mixed[:, :, 2])
    attended = low(low_back(attend(query, keyset, valueset, segment)))
    hidden = low_back(jnp.dot(second, low_up, precision=HIGH, preferred_element_type=jnp.float32) + bias_hidden)
    active = low(jax.nn.gelu(hidden, approximate=False))
    branch = jnp.dot(attended, low_out, precision=HIGH, preferred_element_type=jnp.float32)
    branch = branch + jnp.dot(active, low_down, precision=HIGH, preferred_element_type=jnp.float32)
    return rows_in + branch + gains[4] + gains[5]

def adam_step(weight, grad, first, second, rate, decay):
    first_new = BETA_ONE * first + (1.0 - BETA_ONE) * grad
    second_new = BETA_TWO * second + (1.0 - BETA_TWO) * grad * grad
    first_hat = first_new / (1.0 - BETA_ONE ** STEP)
    second_hat = second_new / (1.0 - BETA_TWO ** STEP)
    weight_new = weight - rate * (first_hat / (jnp.sqrt(second_hat) + ADAM_EPS) + decay * weight)
    return (weight_new, first_new, second_new)

def reference(tokens, cotangent, lengths, w_qkv, w_out, w_up, w_down, norm_vec, b_qkv, b_up, m_qkv, m_out, m_up, m_down, m_norm, m_bqkv, m_bup, v_qkv, v_out, v_up, v_down, v_norm, v_bqkv, v_bup):
    checked = jax.checkpoint(group_forward)

    def forward(token_vals, weight_qkv, weight_out, weight_up, weight_down, gains, bias_mix, bias_hidden):
        low_qkv = low(weight_qkv)
        low_out = low(weight_out)
        low_up = low(weight_up)
        low_down = low(weight_down)

        def group_step(carry, packed):
            rows_in, lengths_row = packed
            return (carry, checked(rows_in, lengths_row, low_qkv, low_out, low_up, low_down, gains, bias_mix, bias_hidden))
        carry, outs = lax.scan(group_step, None, (token_vals.reshape(GROUPS, GROUP_TOK, D), lengths))
        return outs.reshape(TOKENS, D)
    token_vals = tokens.astype(jnp.float32)
    result, pullback = jax.vjp(forward, token_vals, w_qkv, w_out, w_up, w_down, norm_vec, b_qkv, b_up)
    used = lengths[:, 0] + lengths[:, 1]
    live = (jnp.arange(GROUP_TOK, dtype=jnp.int32)[None, :] < used[:, None]).reshape(TOKENS)
    back = cotangent.astype(jnp.float32) * live[:, None].astype(jnp.float32)
    grads = pullback(back)
    layer_out = result.astype(jnp.bfloat16)
    grad_in = grads[0].astype(jnp.bfloat16)
    params = grads[1:]
    total = jnp.float32(0.0)
    for piece in params:
        total = total + jnp.sum(piece * piece)
    grad_norm = jnp.sqrt(total)
    factor = jnp.minimum(1.0, CLIP_NORM / (grad_norm + 1e-06))
    rate_big = 2.5 * D ** (-0.5)
    rate_out = 2.5 * max(16 * D // GROUP_TOK, 1) ** (-0.5)
    weights = (w_qkv, w_out, w_up, w_down, norm_vec, b_qkv, b_up)
    firsts = (m_qkv, m_out, m_up, m_down, m_norm, m_bqkv, m_bup)
    seconds = (v_qkv, v_out, v_up, v_down, v_norm, v_bqkv, v_bup)
    news, moms, secs = ([], [], [])
    for place in range(7):
        if place == 1:
            rate = rate_out
        elif place < 4:
            rate = rate_big
        else:
            rate = RATE_SMALL
        decay = DECAY if place < 4 else 0.0
        weight_new, first_new, second_new = adam_step(weights[place], factor * params[place], firsts[place], seconds[place], rate, decay)
        news.append(weight_new)
        moms.append(first_new)
        secs.append(second_new)
    return (layer_out, grad_in, grad_norm, news[0], news[1], news[2], news[3], news[4], news[5], news[6], moms[0], moms[1], moms[2], moms[3], moms[4], moms[5], moms[6], secs[0], secs[1], secs[2], secs[3], secs[4], secs[5], secs[6])
```

```python
import functools

import jax
import jax.numpy as jnp
from jax import lax
from jax.experimental import pallas as pl
from jax.experimental.pallas import tpu as pltpu
from jax.sharding import Mesh
from jax.sharding import PartitionSpec as P

D = 2048
HD = 128
ROT = 32
GROUP_TOK = 2048
STEP = 10

LN_EPS = 1e-05
ROPE_BASE = 10000.0
CLIP_NORM = 1.0
BETA_ONE = 0.9
BETA_TWO = 0.95
ADAM_EPS = 1e-08
DECAY = 0.01
RATE_SMALL = 1.0

F32 = jnp.float32
BF16 = jnp.bfloat16
MB = 1 << 20
SQRT_HALF = 0.7071067811865476
DENSITY = 0.3989422804014327
SCALE_TWO = HD**-0.5 * 1.4426950408889634

NN = (((1,), (0,)), ((), ()))
NT = (((1,), (1,)), ((), ()))
TN = (((0,), (0,)), ((), ()))


def mm(a, b, dims=NN):
    return lax.dot_general(a, b, dims, preferred_element_type=F32)


def cost(flops, nbytes, trans=0):
    return pl.CostEstimate(flops=int(flops), bytes_accessed=int(nbytes), transcendentals=int(trans))


def params(mib, *sem):
    return pltpu.CompilerParams(
        vmem_limit_bytes=mib * MB, dimension_semantics=sem if sem else None
    )


def shape(dims, dtype):
    return jax.ShapeDtypeStruct(dims, dtype)


HBM = pl.BlockSpec(memory_space=pl.ANY)


def after(value, *earlier):
    return lax.optimization_barrier((value, earlier))[0]


def fetch(table, sources, buf, sem):
    step, last = pl.program_id(0), pl.num_programs(0) - 1
    size = buf.shape[1]

    def start(at):
        slot = lax.rem(at, 2)
        for i, source in enumerate(sources):

            @pl.when(table[at, 1] == i)
            def _(source=source):
                span = pl.ds(pl.multiple_of(table[at, 2] * size, size), size)
                pltpu.make_async_copy(source.at[span], buf.at[slot], sem.at[slot]).start()

    @pl.when(step == 0)
    def _():
        start(step)

    @pl.when(step < last)
    def _():
        start(step + 1)

    slot = lax.rem(step, 2)
    pltpu.make_async_copy(sources[0].at[pl.ds(0, size)], buf.at[slot], sem.at[slot]).wait()
    return slot


def turn(u, cosine, low, high):
    return u * cosine + pltpu.roll(u, HD - ROT // 2, 1) * low + pltpu.roll(u, ROT // 2, 1) * high


def turn_back(g, cosine, low, high):
    return g * cosine - pltpu.roll(g, HD - ROT // 2, 1) * low - pltpu.roll(g, ROT // 2, 1) * high


def enter_kernel(many, units, table, *refs):
    sources = refs[:many]
    vec_ref, w_ref, bu_ref, bq_ref, cos_ref, low_ref, high_ref = refs[many : many + 7]
    xo_ref, a1_ref, a2_ref, stat_ref, act_ref, gp_ref, qkv_ref, buf, sem = refs[-9:]
    slot = fetch(table, sources, buf, sem)
    x_in = buf[slot]
    xo_ref[...] = x_in
    x = x_in.astype(F32)
    mean = jnp.mean(x, axis=1, keepdims=True)
    centre = x - mean
    rstd = lax.rsqrt(jnp.mean(centre * centre, axis=1, keepdims=True) + LN_EPS)
    xhat = centre * rstd
    a1_ref[...] = (xhat * vec_ref[0:1, :] + vec_ref[1:2, :]).astype(BF16)
    a2_ref[...] = (xhat * vec_ref[2:3, :] + vec_ref[3:4, :]).astype(BF16)
    lane = lax.broadcasted_iota(jnp.int32, stat_ref.shape, 1)
    stat_ref[...] = jnp.where(lane == 0, mean, rstd)
    tile = min(1024, units)
    for at in range(0, units, tile):
        span = slice(at, at + tile)
        hidden = mm(a2_ref[...], w_ref[:, span]) + bu_ref[:, span]
        phi_cum = 0.5 + 0.5 * lax.erf(hidden * SQRT_HALF)
        act_ref[:, span] = (hidden * phi_cum).astype(BF16)
        dens = jnp.exp(-0.5 * hidden * hidden) * DENSITY
        gp_ref[:, span] = (phi_cum + hidden * dens).astype(BF16)
    mixed = mm(a1_ref[...], w_ref[:, units:]) + bq_ref[...]
    rotation = (cos_ref[...], low_ref[...], high_ref[...])
    for part in range(mixed.shape[1] // HD):
        piece = mixed[:, part * HD : (part + 1) * HD]
        if part % 3 < 2:
            piece = turn(piece, *rotation)
        qkv_ref[:, part * HD : (part + 1) * HD] = piece.astype(BF16)


def enter(rows, table, sources, norm_vec, w_in, b_up, b_qkv, rotation, old):
    many, steps = len(sources), table.shape[0]
    units, wide = b_up.shape[1], b_qkv.shape[1]
    group = rotation[0].shape[0]
    row = lambda n: pl.BlockSpec((rows, n), lambda i, p: (p[i, 0], 0))
    fixed = lambda v: pl.BlockSpec(v.shape, lambda i, p: (0, 0), pipeline_mode=pl.Buffered(1))
    in_specs = [HBM] * many + [fixed(v) for v in (norm_vec, w_in, b_up, b_qkv)] + [row(HD)] * 3
    args = [table, *sources, norm_vec, w_in, b_up, b_qkv, *rotation]
    widths = ((D, BF16), (D, BF16), (D, BF16), (128, F32), (units, BF16), (units, BF16), (wide, BF16))
    aliases = {}
    if old is not None:
        aliases = {len(args) + i: i for i in range(7)}
        in_specs += [HBM] * 7
        args += list(old)
    return pl.pallas_call(
        functools.partial(enter_kernel, many, units),
        grid_spec=pltpu.PrefetchScalarGridSpec(
            num_scalar_prefetch=1,
            grid=(steps,),
            in_specs=in_specs,
            out_specs=[row(n) for n, _ in widths],
            scratch_shapes=[pltpu.VMEM((2, rows, D), BF16), pltpu.SemaphoreType.DMA((2,))],
        ),
        out_shape=[shape((group, n), kind) for n, kind in widths],
        input_output_aliases=aliases,
        compiler_params=params(60),
        cost_estimate=cost(2 * steps * rows * D * (units + wide), 2 * D * (units + wide)),
        name="enter",
    )(*args)


def masked(scores, at, cases, width, begin):
    key_at = lax.broadcasted_iota(jnp.int32, (width, width), 0)
    query_at = lax.broadcasted_iota(jnp.int32, (width, width), 1)
    ok = key_at <= query_at
    if at == cases - 1:
        ok = ok & (key_at + at * width >= begin)
    return jnp.where(ok, scores, -jnp.inf)


def fwd_case(at, cases, width, q_ref, k_ref, v_ref, begin_ref, o_ref, lse_ref):
    first = at * width
    query, begin = q_ref[...], begin_ref[...]
    near = masked(mm(k_ref[first : first + width, :], query, NT), at, cases, width, begin)
    top = jnp.max(near, axis=0, keepdims=True)
    if at:
        far = mm(k_ref[0:first, :], query, NT)
        if at == cases - 1:
            far = far + jnp.where(begin > 0, -jnp.inf, 0.0)
        top = jnp.maximum(top, jnp.max(far, axis=0, keepdims=True))
    near = jnp.exp2((near - top) * SCALE_TWO)
    total = jnp.sum(near, axis=0, keepdims=True)
    if at:
        far = jnp.exp2((far - top) * SCALE_TWO)
        total = total + jnp.sum(far, axis=0, keepdims=True)
    part = 1.0 / total
    out = mm(v_ref[first : first + width, :], (near * part).astype(BF16), TN)
    if at:
        out = out + mm(v_ref[0:first, :], (far * part).astype(BF16), TN)
    o_ref[...] = out.T.astype(BF16)
    lse_ref[0] = top * SCALE_TWO + jnp.log2(total)


def attn_fwd_kernel(cases, width, q_ref, k_ref, v_ref, begin_ref, *rest):
    o_ref, lse_ref = rest[-2:]
    for at in range(cases):

        @pl.when(pl.program_id(1) == at)
        def _(at=at):
            fwd_case(at, cases, width, q_ref, k_ref, v_ref, begin_ref, o_ref, lse_ref)


def attn_fwd(first, count, qkv, begin, old):
    group = qkv.shape[0]
    heads = qkv.shape[1] // (3 * HD)
    width = min(1024, group)
    cases = group // width
    flops = 2 * 2 * count * group * group * HD * 5 // 8
    in_specs = [
        pl.BlockSpec((width, HD), lambda h, i: (i, 3 * (first + h))),
        pl.BlockSpec((group, HD), lambda h, i: (0, 3 * (first + h) + 1)),
        pl.BlockSpec((group, HD), lambda h, i: (0, 3 * (first + h) + 2)),
        pl.BlockSpec((1, width), lambda h, i: (0, i)),
    ]
    args, aliases = [qkv, qkv, qkv, begin], {}
    if old is not None:
        aliases = {len(args) + i: i for i in range(2)}
        in_specs += [HBM] * 2
        args += list(old)
    return pl.pallas_call(
        functools.partial(attn_fwd_kernel, cases, width),
        grid=(count, cases),
        in_specs=in_specs,
        out_specs=[
            pl.BlockSpec((width, HD), lambda h, i: (i, first + h)),
            pl.BlockSpec((1, 1, width), lambda h, i: (first + h, 0, i)),
        ],
        out_shape=[shape((group, heads * HD), BF16), shape((heads, 1, group), F32)],
        input_output_aliases=aliases,
        compiler_params=params(56),
        cost_estimate=cost(4 * flops, 8 * group * count * HD, count * group * group * 5 // 8),
        name="attend",
    )(*args)


def bwd_case(at, cases, width, refs):
    (q_ref, k_ref, v_ref, do_ref, begin_ref, lse_ref, dk_acc, dv_acc) = refs
    first = at * width
    query, dctx, begin, lse = q_ref[...], do_ref[...], begin_ref[...], lse_ref[0]
    spans = [slice(first, first + width)] + ([slice(0, first)] if at else [])
    parts = []
    for span in spans:
        scores = mm(k_ref[span, :], query, NT) * SCALE_TWO - lse
        if span.start == first:
            scores = masked(scores, at, cases, width, begin)
        elif at == cases - 1:
            scores = scores + jnp.where(begin > 0, -jnp.inf, 0.0)
        prob = jnp.exp2(scores)
        dprob = mm(v_ref[span, :], dctx, NT)
        parts.append((span, prob, dprob, jnp.sum(prob * dprob, axis=0, keepdims=True)))
    inner = sum(p[3] for p in parts)
    dq = None
    for span, prob, dprob, _ in parts:
        dscores = (prob * (dprob - inner)).astype(BF16)
        dv_acc[span, :] += mm(prob.astype(BF16), dctx)
        dk_acc[span, :] += mm(dscores, query)
        more = mm(k_ref[span, :], dscores, TN)
        dq = more if dq is None else dq + more
    return dq.T


def attn_bwd_kernel(
    cases, width, q_ref, k_ref, v_ref, do_ref, begin_ref, lse_ref, cos_ref, low_ref, high_ref,
    out_ref, sum_ref, dk_acc, dv_acc,
):
    step = pl.program_id(1)

    @pl.when(step == 0)
    def _():
        dk_acc[...] = jnp.zeros_like(dk_acc)
        dv_acc[...] = jnp.zeros_like(dv_acc)

    refs = (q_ref, k_ref, v_ref, do_ref, begin_ref, lse_ref, dk_acc, dv_acc)
    for at in range(cases):

        @pl.when(step == at)
        def _(at=at):
            dq = bwd_case(at, cases, width, refs) * (HD**-0.5)
            span = slice(at * width, (at + 1) * width)
            back = turn_back(dq, cos_ref[span, :], low_ref[span, :], high_ref[span, :])
            out_ref[span, 0:HD] = back.astype(BF16)

    @pl.when(step == cases - 1)
    def _():
        dk = dk_acc[...] * (HD**-0.5)
        back = turn_back(dk, cos_ref[...], low_ref[...], high_ref[...])
        out_ref[:, HD : 2 * HD] = back.astype(BF16)
        out_ref[:, 2 * HD : 3 * HD] = dv_acc[...].astype(BF16)
        total = jnp.sum(out_ref[...].astype(F32), axis=0, keepdims=True)
        sum_ref[...] = jnp.broadcast_to(total, sum_ref.shape)


def attn_bwd(qkv, dctx, begin, lse, tables):
    group = qkv.shape[0]
    heads = qkv.shape[1] // (3 * HD)
    width = min(512, group)
    cases = group // width
    table = pl.BlockSpec((group, HD), lambda h, i: (0, 0))
    flops = 5 * 2 * heads * group * group * HD * 5 // 8
    return pl.pallas_call(
        functools.partial(attn_bwd_kernel, cases, width),
        grid=(heads, cases),
        in_specs=[
            pl.BlockSpec((width, HD), lambda h, i: (i, 3 * h)),
            pl.BlockSpec((group, HD), lambda h, i: (0, 3 * h + 1)),
            pl.BlockSpec((group, HD), lambda h, i: (0, 3 * h + 2)),
            pl.BlockSpec((width, HD), lambda h, i: (i, h)),
            pl.BlockSpec((1, width), lambda h, i: (0, i)),
            pl.BlockSpec((1, 1, width), lambda h, i: (h, 0, i)),
            table,
            table,
            table,
        ],
        out_specs=[
            pl.BlockSpec((group, 3 * HD), lambda h, i: (0, h)),
            pl.BlockSpec((8, 3 * HD), lambda h, i: (0, h)),
        ],
        out_shape=[shape((group, heads * 3 * HD), BF16), shape((8, heads * 3 * HD), F32)],
        scratch_shapes=[pltpu.VMEM((group, HD), F32), pltpu.VMEM((group, HD), F32)],
        compiler_params=params(56),
        cost_estimate=cost(flops / 2, 3 * group * heads * HD),
        name="attend_back",
    )(qkv, qkv, qkv, dctx, begin, lse, *tables)


def branch_kernel(units, o_ref, act_ref, w_ref, out_ref):
    total = mm(act_ref[...], w_ref[0:units, :]) + mm(o_ref[...], w_ref[units:, :])
    out_ref[...] = total.astype(BF16)


def branch_all(o, act, w_back):
    group, heads, units = o.shape[0], o.shape[1], act.shape[1]
    rows, tile = 512, D // 2
    return pl.pallas_call(
        functools.partial(branch_kernel, units),
        grid=(D // tile, group // rows),
        in_specs=[
            pl.BlockSpec((rows, heads), lambda j, i: (i, 0)),
            pl.BlockSpec((rows, units), lambda j, i: (i, 0)),
            pl.BlockSpec((heads + units, tile), lambda j, i: (0, j)),
        ],
        out_specs=pl.BlockSpec((rows, tile), lambda j, i: (i, j)),
        out_shape=shape((group, D), BF16),
        compiler_params=params(56),
        cost_estimate=cost(2 * group * D * (heads + units), 2 * D * (heads + units)),
        name="branch",
    )(o, act, w_back)


def leave_kernel(many, units, table, *refs):
    sources, (w_ref, gp_ref) = refs[:many], refs[many : many + 2]
    eo_ref, dh_ref, do_ref, sum_ref, buf, sem = refs[-6:]
    slot = fetch(table, sources, buf, sem)

    @pl.when(pl.program_id(0) == 0)
    def _():
        sum_ref[...] = jnp.zeros_like(sum_ref)

    back = buf[slot]
    eo_ref[...] = back
    tile = min(1024, units)
    for at in range(0, units, tile):
        span = slice(at, at + tile)
        dact = mm(back, w_ref[span, :], NT)
        dhid = (dact * gp_ref[:, span].astype(F32)).astype(BF16)
        dh_ref[:, span] = dhid
        total = jnp.sum(dhid.astype(F32), axis=0, keepdims=True)
        sum_ref[:, span] += jnp.broadcast_to(total, (8, tile))
    do_ref[...] = mm(back, w_ref[units:, :], NT).astype(BF16)


def leave(rows, table, sources, w_back, gp, old):
    many, steps = len(sources), table.shape[0]
    group, units = gp.shape
    heads = w_back.shape[0] - units
    row = lambda n: pl.BlockSpec((rows, n), lambda i, p: (p[i, 0], 0))
    in_specs = [HBM] * many + [
        pl.BlockSpec(w_back.shape, lambda i, p: (0, 0), pipeline_mode=pl.Buffered(1)),
        row(units),
    ]
    args = [table, *sources, w_back, gp]
    aliases = {}
    if old is not None:
        aliases = {len(args) + i: i for i in range(3)}
        in_specs += [HBM] * 3
        args += list(old)
    return pl.pallas_call(
        functools.partial(leave_kernel, many, units),
        grid_spec=pltpu.PrefetchScalarGridSpec(
            num_scalar_prefetch=1,
            grid=(steps,),
            in_specs=in_specs,
            out_specs=[row(D), row(units), row(heads), pl.BlockSpec((8, units), lambda i, p: (0, 0))],
            scratch_shapes=[pltpu.VMEM((2, rows, D), BF16), pltpu.SemaphoreType.DMA((2,))],
        ),
        out_shape=[
            shape((group, D), BF16),
            shape((group, units), BF16),
            shape((group, heads), BF16),
            shape((8, units), F32),
        ],
        input_output_aliases=aliases,
        compiler_params=params(60),
        cost_estimate=cost(2 * steps * rows * D * (units + heads), 2 * D * (units + heads)),
        name="leave",
    )(*args)


def din_kernel(dm_ref, dh_ref, w_ref, x_ref, stat_ref, vec_ref, g_ref, sum_ref):
    units = dh_ref.shape[1]
    left = mm(dm_ref[...], w_ref[:, units:], NT)
    right = mm(dh_ref[...], w_ref[:, 0:units], NT)
    g_ref[...] = (left * vec_ref[0:1, :] + right * vec_ref[2:3, :]).astype(BF16)
    xhat = (x_ref[...].astype(F32) - stat_ref[:, 0:1]) * stat_ref[:, 1:2]
    rows = [left * xhat, left, right * xhat, right]
    sums = jnp.concatenate(
        [jnp.sum(r, axis=0, keepdims=True) for r in rows] + [jnp.zeros((4, left.shape[1]), F32)], axis=0
    )

    @pl.when(pl.program_id(1) == 0)
    def _():
        sum_ref[...] = sums

    @pl.when(pl.program_id(1) > 0)
    def _():
        sum_ref[...] += sums


def din_all(dmixed, dhid, w_in, x, stat, norm_vec):
    group, heads3, units = dmixed.shape[0], dmixed.shape[1], dhid.shape[1]
    rows, tile = 512, 1024
    return pl.pallas_call(
        din_kernel,
        grid=(D // tile, group // rows),
        in_specs=[
            pl.BlockSpec((rows, heads3), lambda j, i: (i, 0)),
            pl.BlockSpec((rows, units), lambda j, i: (i, 0)),
            pl.BlockSpec((tile, heads3 + units), lambda j, i: (j, 0)),
            pl.BlockSpec((rows, tile), lambda j, i: (i, j)),
            pl.BlockSpec((rows, 128), lambda j, i: (i, 0)),
            pl.BlockSpec((6, tile), lambda j, i: (0, j)),
        ],
        out_specs=[
            pl.BlockSpec((rows, tile), lambda j, i: (i, j)),
            pl.BlockSpec((8, tile), lambda j, i: (0, j)),
        ],
        out_shape=[shape((group, D), BF16), shape((8, D), F32)],
        compiler_params=params(60),
        cost_estimate=cost(group * D * (heads3 + units) / 2, D * (heads3 + units) / 2),
        name="input_back",
    )(dmixed, dhid, w_in, x, stat, norm_vec)


def wgrad_kernel(n_left, n_right, cut_left, many, place, *refs):
    lefts, rights = refs[:n_left], refs[n_left : n_left + n_right]
    rest = refs[n_left + n_right :]
    got, outs = (rest[0], rest[1:]) if len(rest) > many else (None, rest)
    pairs = list(zip(lefts, rights)) if cut_left else [(v, rights[0]) for v in lefts]
    values = [mm(a[...], b[...], TN) for a, b in pairs]
    axis = 1 if cut_left else 0

    def put(ref):
        at = 0
        for value in values:
            span = slice(at, at + value.shape[axis])
            at += value.shape[axis]
            view = (0, slice(None), span) if cut_left else (0, span, slice(None))
            if got is not None:
                value = value + got[view].astype(F32)
            ref[view] = value.astype(BF16)

    if many == 1:
        put(outs[0])
    else:
        for i in range(many):

            @pl.when(pl.program_id(0) == i)
            def _(i=i):
                put(outs[i])


def wgrad(lefts, rights, cut_left, weight, place, quads, got):
    rows = lefts[0].shape[0]
    whole = lambda n: pl.BlockSpec((rows, n), lambda i, p: (0, 0), pipeline_mode=pl.Buffered(1))
    part = lambda n: pl.BlockSpec((rows, n // (2 * quads)), lambda i, p: (0, 2 * (i ^ p[1]) + p[0]))
    widths = [v.shape[1] for v in lefts], [v.shape[1] for v in rights]
    if cut_left:
        in_specs = [part(n) for n in widths[0]] + [whole(n) for n in widths[1]]
        tile = (widths[0][0] // (2 * quads), sum(widths[1]))
    else:
        in_specs = [whole(n) for n in widths[0]] + [part(n) for n in widths[1]]
        tile = (sum(widths[0]), widths[1][0] // (2 * quads))
    args = [place, *lefts, *rights]
    stacked = pl.BlockSpec((1, *tile), lambda i, p: (i, 0, 0))
    if got is None:
        out_specs, out_shape = [stacked], [shape((quads, *tile), BF16)]
    else:
        in_specs.append(stacked)
        args.append(got)
        out_specs = [
            pl.BlockSpec((1, *tile), lambda i, p: (0, 0, 0), pipeline_mode=pl.Buffered(1))
        ] * quads
        out_shape = [shape((1, *tile), BF16)] * quads
    flops = rows * tile[0] * tile[1] * 2 * quads * weight
    return pl.pallas_call(
        functools.partial(wgrad_kernel, len(lefts), len(rights), cut_left, len(out_specs)),
        grid_spec=pltpu.PrefetchScalarGridSpec(
            num_scalar_prefetch=1, grid=(quads,), in_specs=in_specs, out_specs=out_specs
        ),
        out_shape=out_shape,
        compiler_params=params(60),
        cost_estimate=cost(flops, 2 * rows * sum(widths[0] + widths[1])),
        name="weight_grad",
    )(*args)


def part_kernel(n_left, turns, size, place, *refs):
    lefts, rights, rest = refs[:n_left], refs[n_left : n_left + turns], refs[n_left + turns :]
    base_ref = rest[0] if len(rest) == 4 else None
    out_ref, rows_ref, sem = rest[-3:]

    @pl.when(pl.program_id(0) == 0)
    def _():
        copies, at = [], 0
        for i, left in enumerate(lefts):
            span = slice(at, at + left.shape[1])
            at += left.shape[1]
            for k in range(turns):
                source = left.at[pl.ds(pl.multiple_of(place[2 + k] * size, size), size)]
                target = rows_ref.at[k * size : (k + 1) * size, span]
                copies.append(pltpu.make_async_copy(source, target, sem.at[i, k]))
        for copy in copies:
            copy.start()
        for copy in copies:
            copy.wait()

    right = jnp.concatenate([r[...] for r in rights], axis=0) if turns > 1 else rights[0][...]
    value = mm(rows_ref[...], right, TN)
    if base_ref is not None:
        value = value + base_ref[0]
    out_ref[0] = value.astype(out_ref.dtype)


def wgrad_part(lefts, right, size, place, turns, quads, base):
    widths = [v.shape[1] for v in lefts]
    tile = (sum(widths), right.shape[1] // (2 * quads))
    in_specs = [HBM] * len(lefts) + [
        pl.BlockSpec((size, tile[1]), lambda i, p, k=k: (p[2 + k], 2 * (i ^ p[1]) + p[0]))
        for k in range(turns)
    ]
    args = [place, *lefts] + [right] * turns
    stacked = pl.BlockSpec((1, *tile), lambda i, p: (i, 0, 0))
    if base is not None:
        in_specs.append(stacked)
        args.append(base)
    return pl.pallas_call(
        functools.partial(part_kernel, len(lefts), turns, size),
        grid_spec=pltpu.PrefetchScalarGridSpec(
            num_scalar_prefetch=1,
            grid=(quads,),
            in_specs=in_specs,
            out_specs=stacked,
            scratch_shapes=[
                pltpu.VMEM((turns * size, tile[0]), BF16),
                pltpu.SemaphoreType.DMA((len(lefts), turns)),
            ],
        ),
        out_shape=shape((quads, *tile), F32 if base is None else BF16),
        compiler_params=params(60),
        cost_estimate=cost(size * turns * tile[0] * tile[1] * 2 * quads, 0),
        name="weight_grad_part",
    )(*args)


def line_turns(count):
    table = []
    for place in range(count):
        order = []
        for step in range(1, count):
            if place - step >= 0:
                order.append((True, step))
            if place + step < count:
                order.append((False, step))
        table.append(order)
    return table


def lookup(table, place):
    return jnp.asarray(table, jnp.int32)[place]


class Gather:
    def __init__(self, pieces, count, place):
        self.right, self.left = [[v] for v in pieces], [[v] for v in pieces]
        self.count, self.place = count, place

    def step(self, piece, *earlier):
        count, right, left = self.count, self.right[piece], self.left[piece]
        step = len(right)
        here, there = after((right[-1], left[-1]), *earlier)
        right.append(lax.ppermute(here, "mp", [(i, i + 1) for i in range(step - 1, count - 1)]))
        left.append(lax.ppermute(there, "mp", [(i + 1, i) for i in range(0, count - step)]))

    def last(self):
        return [(r[-1], l[-1]) for r, l in zip(self.right, self.left)]

    def turns(self, first, last, size):
        count, many = self.count, len(self.right)
        each = self.right[0][0].shape[0] // size
        turns = line_turns(count)
        sources, tables = [], [[] for _ in range(count)]
        for turn_at in range(first, last + 1):
            for piece in range(many):
                for i in range(count):
                    side, far = turns[i][turn_at - 1] if turn_at else (True, 0)
                    key = (side, far, piece)
                    if key not in sources:
                        sources.append(key)
                    at = (i - far if side else i + far) * many + piece
                    tables[i] += [[at * each + k, sources.index(key), k] for k in range(each)]
        arrays = [(self.right if side else self.left)[piece][far] for side, far, piece in sources]
        return lookup(tables, self.place), arrays


def everywhere(value, axes):
    for axis, size in axes:
        hop = 1
        while hop < size:
            value = value + lax.ppermute(value, axis, [(i, i ^ hop) for i in range(size)])
            hop *= 2
    return value


def adam_step(weight, grad, first, second, rate, decay):
    first_new = BETA_ONE * first + (1.0 - BETA_ONE) * grad
    second_new = BETA_TWO * second + (1.0 - BETA_TWO) * grad * grad
    first_hat = first_new / (1.0 - BETA_ONE**STEP)
    second_hat = second_new / (1.0 - BETA_TWO**STEP)
    weight_new = weight - rate * (first_hat / (jnp.sqrt(second_hat) + ADAM_EPS) + decay * weight)
    return (weight_new, first_new, second_new)


def rotation_tables(position):
    half = ROT // 2
    inverse = ROPE_BASE ** (-jnp.arange(half, dtype=F32) * 2.0 / ROT)
    angle = position[:, None] * inverse[None, :]
    cosine, sine = jnp.cos(angle), jnp.sin(angle)
    rows = position.shape[0]
    rest = jnp.zeros((rows, HD - ROT), F32)
    zero = jnp.zeros((rows, half), F32)
    return (
        jnp.concatenate([cosine, cosine, rest + 1.0], axis=1),
        jnp.concatenate([-sine, zero, rest], axis=1),
        jnp.concatenate([zero, sine, rest], axis=1),
    )


def local(
    tokens, cotangent, lengths, w_qkv, w_out, w_up, w_down, norm_vec, b_qkv, b_up,
    m_qkv, m_out, m_up, m_down, m_norm, m_bqkv, m_bup,
    v_qkv, v_out, v_up, v_down, v_norm, v_bqkv, v_bup,
):
    rows = tokens.shape[0]
    count = lax.axis_size("mp")
    quads = lax.axis_size("quad")
    place = lax.axis_index("mp")
    core = lax.axis_index("pair")
    group = rows * count
    dp = ("quad", "pair")

    first_len = lengths[0, 0]
    used = lengths[0, 0] + lengths[0, 1]
    row_ids = jnp.arange(group, dtype=jnp.int32)
    begin = jnp.where(row_ids >= used, used, jnp.where(row_ids >= first_len, first_len, 0))
    begin = begin.astype(jnp.int32)
    tables = rotation_tables((row_ids - begin).astype(F32))
    begin = begin.reshape(1, group)
    own_ids = jnp.arange(rows, dtype=jnp.int32) + place * rows
    live_own = (own_ids < used).astype(BF16)

    sub = min(256, rows)
    back_own = cotangent * live_own[:, None]
    x_line = Gather([tokens], count, place)
    x_line.step(0)
    full_in = jnp.concatenate([w_up.astype(BF16), w_qkv.astype(BF16)], axis=1)
    full_in = lax.all_gather(full_in, dp, axis=0, tiled=True)
    late_down, late_out = after((w_down, w_out), x_line.last()[0])
    full_back = jnp.concatenate([late_down.astype(BF16), late_out.astype(BF16)], axis=0)
    full_back = lax.all_gather(full_back, dp, axis=1, tiled=True)
    b_up_row, b_qkv_row = b_up.reshape(1, -1), b_qkv.reshape(1, -1)

    for step in range(2, count):
        x_line.step(0)
    enter_rest = (norm_vec, full_in, b_up_row, b_qkv_row, tables)
    table, sources = x_line.turns(0, count - 2, sub)
    state = enter(sub, table, sources, *enter_rest, None)
    e_line = Gather([after(back_own, state[0])], count, place)
    e_line.step(0)
    table, sources = x_line.turns(count - 1, count - 1, sub)
    table = after(table, state, x_line.last())
    state = enter(sub, table, sources, *enter_rest, state)
    x_all, a1, a2, stat, act, gelu_slope, qkv = state

    heads = qkv.shape[1] // (3 * HD)
    attended = attn_fwd(0, heads // 2, qkv, begin, None)
    e_line.step(0, attended[0])
    attended, lse = attn_fwd(heads // 2, heads - heads // 2, qkv, begin, attended)
    parts = branch_all(attended, act, full_back)

    def leave_at(first, last, old, *earlier):
        table, sources = e_line.turns(first, last, sub)
        old = None if old is None else old[:3]
        return leave(sub, after(table, *earlier), sources, full_back, gelu_slope, old)

    for step in range(3, count):
        e_line.step(0, parts)
    one = leave_at(0, 1, None, parts)
    two = leave_at(2, count - 2, one, one)
    quad = lax.axis_index("quad")
    here = jnp.stack([core, quad]).astype(jnp.int32)
    there = jnp.stack([1 - core, quad]).astype(jnp.int32)
    arrival = lookup(
        [[i] + [i - far if side else i + far for side, far in line_turns(count)[i]] for i in range(count)],
        place,
    )
    second = (act, attended)
    early = jnp.concatenate([there, arrival[: count - 1]])
    give_second = wgrad_part(second, two[0], rows, after(early, two[1]), count - 1, quads, None)
    three = leave_at(count - 1, count - 1, two, give_second, e_line.last())
    back_rows, dhid, dctx = three[:3]
    grad_bup = (one[3] + two[3] + three[3])[0]
    parts = after(parts, give_second, e_line.last())
    branch = lax.psum_scatter(parts, "mp", scatter_dimension=0, tiled=True)

    def give(product, *earlier):
        half = wgrad(*product, after(there, *earlier), quads, None)[0]
        return lax.ppermute(half, "pair", [(0, 1), (1, 0)]), half

    def settle(product, got, *earlier):
        blocks = wgrad(*product, after(here, *earlier), quads, got)
        terms = [
            lax.ppermute(blocks[hop], "quad", [(i, i ^ hop) for i in range(quads)])
            for hop in range(1, quads)
        ]
        return [blocks[0]] + terms

    def total(terms):
        return sum(v[0].astype(F32) for v in terms)

    up = ((a2,), (dhid,), True, 0.05)
    late = jnp.concatenate([there, arrival[count - 1 :]])
    mark = wgrad_part(second, back_rows, rows, after(late, dhid), 1, quads, give_second)
    got_second = lax.ppermute(mark, "pair", [(0, 1), (1, 0)])
    got_up, mark = give(up, mark)
    sum_second = settle((second, (back_rows,), False, 0.25), got_second, mark)
    dmixed, col_qkv = attn_bwd(qkv, dctx, after(begin, sum_second[0]), lse, tables)
    grad_bqkv = col_qkv[0]
    inner = ((a1,), (dmixed,), True, 9)
    sum_up = settle(up, got_up, dmixed)
    grad_parts, col = din_all(
        after(dmixed, sum_up[0], *sum_second[1:]), dhid, full_in, x_all, stat, norm_vec
    )
    grad_rows = lax.psum_scatter(grad_parts, "mp", scatter_dimension=0, tiled=True).astype(F32)

    back_vals = back_own.astype(F32)
    out_bias = jnp.sum(back_vals, axis=0)
    small = jnp.concatenate([col[0:4], out_bias[None], out_bias[None]], axis=0)
    packed = jnp.concatenate([small.reshape(-1), grad_bqkv, grad_bup]).reshape(-1, 128)
    got_inner, mark = give(inner, grad_parts, branch, *sum_up[1:])
    packed = everywhere(packed, (("pair", 2),))
    sum_inner = settle(inner, got_inner, mark, packed)
    packed = everywhere(packed, (("quad", quads),))
    part_up, part_qkv, sum_second = total(sum_up), total(sum_inner), total(sum_second)
    units = act.shape[1]
    part_down, part_out = sum_second[:units], sum_second[units:]
    token_vals = tokens.astype(F32)
    layer_out = (token_vals + branch.astype(F32) + norm_vec[4] + norm_vec[5]).astype(BF16)

    n_small = small.size // 128
    n_qkv = grad_bqkv.size // 128
    small_sum = everywhere(packed[:n_small], (("mp", count),))
    grad_small = small_sum.reshape(6, D)
    sum_bqkv = packed[n_small : n_small + n_qkv].reshape(-1)
    sum_bup = packed[n_small + n_qkv :].reshape(-1)

    mean, rstd = (lax.dynamic_slice_in_dim(stat, place * rows, rows, 0)[:, i : i + 1] for i in (0, 1))
    xhat = (token_vals - mean) * rstd
    grad_in = back_vals + rstd * (
        grad_rows
        - jnp.mean(grad_rows, axis=1, keepdims=True)
        - xhat * jnp.mean(grad_rows * xhat, axis=1, keepdims=True)
    )
    grad_in = grad_in.astype(BF16)

    local_squares = (
        jnp.sum(part_qkv * part_qkv)
        + jnp.sum(part_out * part_out)
        + jnp.sum(part_up * part_up)
        + jnp.sum(part_down * part_down)
        + (jnp.sum(sum_bqkv * sum_bqkv) + jnp.sum(sum_bup * sum_bup)) / (2 * quads)
    )
    total = everywhere(
        jnp.broadcast_to(local_squares, (8, 128)), (("pair", 2), ("quad", quads), ("mp", count))
    )[0, 0]
    grad_norm = jnp.sqrt(total + jnp.sum(grad_small * grad_small))
    factor = jnp.minimum(1.0, CLIP_NORM / (grad_norm + 1e-06))
    rate_big = 2.5 * D ** (-0.5)
    rate_out = 2.5 * max(16 * D // GROUP_TOK, 1) ** (-0.5)
    upd_qkv, mom_qkv, sec_qkv = adam_step(w_qkv, factor * part_qkv, m_qkv, v_qkv, rate_big, DECAY)
    upd_out, mom_out, sec_out = adam_step(w_out, factor * part_out, m_out, v_out, rate_out, DECAY)
    upd_up, mom_up, sec_up = adam_step(w_up, factor * part_up, m_up, v_up, rate_big, DECAY)
    upd_down, mom_down, sec_down = adam_step(
        w_down, factor * part_down, m_down, v_down, rate_big, DECAY
    )
    upd_norm, mom_norm, sec_norm = adam_step(
        norm_vec, factor * grad_small, m_norm, v_norm, RATE_SMALL, 0.0
    )
    upd_bqkv, mom_bqkv, sec_bqkv = adam_step(
        b_qkv, factor * sum_bqkv, m_bqkv, v_bqkv, RATE_SMALL, 0.0
    )
    upd_bup, mom_bup, sec_bup = adam_step(b_up, factor * sum_bup, m_bup, v_bup, RATE_SMALL, 0.0)
    return (
        layer_out, grad_in, grad_norm,
        upd_qkv, upd_out, upd_up, upd_down, upd_norm, upd_bqkv, upd_bup,
        mom_qkv, mom_out, mom_up, mom_down, mom_norm, mom_bqkv, mom_bup,
        sec_qkv, sec_out, sec_up, sec_down, sec_norm, sec_bqkv, sec_bup,
    )


def solution(mesh):
    devices = mesh.devices
    split = Mesh(
        devices.reshape(devices.shape[0] // 2, 2, devices.shape[1]), ("quad", "pair", "mp")
    )
    dp = ("quad", "pair")
    tok, row, col = P(("quad", "pair", "mp"), None), P(dp, "mp"), P("mp", dp)
    weights = (row, col, row, col, P(), P("mp"), P("mp"))
    return jax.shard_map(
        local,
        mesh=split,
        in_specs=(tok, tok, P(dp, None)) + weights * 3,
        out_specs=(tok, tok, P()) + weights * 3,
        check_vma=False,
    )
```

```python
import functools

import jax
import jax.numpy as jnp
from jax import lax
from jax.experimental import pallas as pl
from jax.experimental.pallas import tpu as pltpu
from jax.sharding import Mesh
from jax.sharding import PartitionSpec as P

D = 2048
HD = 128
ROT = 32
GROUP_TOK = 2048
STEP = 10

LN_EPS = 1e-05
ROPE_BASE = 10000.0
CLIP_NORM = 1.0
BETA_ONE = 0.9
BETA_TWO = 0.95
ADAM_EPS = 1e-08
DECAY = 0.01
RATE_SMALL = 1.0

F32 = jnp.float32
BF16 = jnp.bfloat16
MB = 1 << 20
SQRT_HALF = 0.7071067811865476
DENSITY = 0.3989422804014327
SCALE_TWO = HD**-0.5 * 1.4426950408889634

NN = (((1,), (0,)), ((), ()))
NT = (((1,), (1,)), ((), ()))
TN = (((0,), (0,)), ((), ()))


def mm(a, b, dims=NN):
    return lax.dot_general(a, b, dims, preferred_element_type=F32)


def cost(flops, nbytes, trans=0):
    return pl.CostEstimate(flops=int(flops), bytes_accessed=int(nbytes), transcendentals=int(trans))


def params(mib, *sem):
    return pltpu.CompilerParams(
        vmem_limit_bytes=mib * MB, dimension_semantics=sem if sem else None
    )


def shape(dims, dtype):
    return jax.ShapeDtypeStruct(dims, dtype)


HBM = pl.BlockSpec(memory_space=pl.ANY)


def after(value, *earlier):
    return lax.optimization_barrier((value, earlier))[0]


def fetch(table, sources, buf, sem):
    step, last = pl.program_id(0), pl.num_programs(0) - 1
    size = buf.shape[1]

    def start(at):
        slot = lax.rem(at, 2)
        for i, source in enumerate(sources):

            @pl.when(table[at, 1] == i)
            def _(source=source):
                span = pl.ds(pl.multiple_of(table[at, 2] * size, size), size)
                pltpu.make_async_copy(source.at[span], buf.at[slot], sem.at[slot]).start()

    @pl.when(step == 0)
    def _():
        start(step)

    @pl.when(step < last)
    def _():
        start(step + 1)

    slot = lax.rem(step, 2)
    pltpu.make_async_copy(sources[0].at[pl.ds(0, size)], buf.at[slot], sem.at[slot]).wait()
    return slot


def turn(u, cosine, low, high):
    return u * cosine + pltpu.roll(u, HD - ROT // 2, 1) * low + pltpu.roll(u, ROT // 2, 1) * high


def turn_back(g, cosine, low, high):
    return g * cosine - pltpu.roll(g, HD - ROT // 2, 1) * low - pltpu.roll(g, ROT // 2, 1) * high


def enter_kernel(many, units, table, *refs):
    sources = refs[:many]
    vec_ref, w_ref, bu_ref, bq_ref, cos_ref, low_ref, high_ref = refs[many : many + 7]
    xo_ref, a1_ref, a2_ref, stat_ref, act_ref, gp_ref, qkv_ref, buf, sem = refs[-9:]
    slot = fetch(table, sources, buf, sem)
    x_in = buf[slot]
    xo_ref[...] = x_in
    x = x_in.astype(F32)
    mean = jnp.mean(x, axis=1, keepdims=True)
    centre = x - mean
    rstd = lax.rsqrt(jnp.mean(centre * centre, axis=1, keepdims=True) + LN_EPS)
    xhat = centre * rstd
    a1_ref[...] = (xhat * vec_ref[0:1, :] + vec_ref[1:2, :]).astype(BF16)
    a2_ref[...] = (xhat * vec_ref[2:3, :] + vec_ref[3:4, :]).astype(BF16)
    lane = lax.broadcasted_iota(jnp.int32, stat_ref.shape, 1)
    stat_ref[...] = jnp.where(lane == 0, mean, rstd)
    tile = min(1024, units)
    for at in range(0, units, tile):
        span = slice(at, at + tile)
        hidden = mm(a2_ref[...], w_ref[:, span]) + bu_ref[:, span]
        phi_cum = 0.5 + 0.5 * lax.erf(hidden * SQRT_HALF)
        act_ref[:, span] = (hidden * phi_cum).astype(BF16)
        dens = jnp.exp(-0.5 * hidden * hidden) * DENSITY
        gp_ref[:, span] = (phi_cum + hidden * dens).astype(BF16)
    mixed = mm(a1_ref[...], w_ref[:, units:]) + bq_ref[...]
    rotation = (cos_ref[...], low_ref[...], high_ref[...])
    for part in range(mixed.shape[1] // HD):
        piece = mixed[:, part * HD : (part + 1) * HD]
        if part % 3 < 2:
            piece = turn(piece, *rotation)
        qkv_ref[:, part * HD : (part + 1) * HD] = piece.astype(BF16)


def enter(rows, table, sources, norm_vec, w_in, b_up, b_qkv, rotation, old):
    many, steps = len(sources), table.shape[0]
    units, wide = b_up.shape[1], b_qkv.shape[1]
    group = rotation[0].shape[0]
    row = lambda n: pl.BlockSpec((rows, n), lambda i, p: (p[i, 0], 0))
    fixed = lambda v: pl.BlockSpec(v.shape, lambda i, p: (0, 0), pipeline_mode=pl.Buffered(1))
    in_specs = [HBM] * many + [fixed(v) for v in (norm_vec, w_in, b_up, b_qkv)] + [row(HD)] * 3
    args = [table, *sources, norm_vec, w_in, b_up, b_qkv, *rotation]
    widths = ((D, BF16), (D, BF16), (D, BF16), (128, F32), (units, BF16), (units, BF16), (wide, BF16))
    aliases = {}
    if old is not None:
        aliases = {len(args) + i: i for i in range(7)}
        in_specs += [HBM] * 7
        args += list(old)
    return pl.pallas_call(
        functools.partial(enter_kernel, many, units),
        grid_spec=pltpu.PrefetchScalarGridSpec(
            num_scalar_prefetch=1,
            grid=(steps,),
            in_specs=in_specs,
            out_specs=[row(n) for n, _ in widths],
            scratch_shapes=[pltpu.VMEM((2, rows, D), BF16), pltpu.SemaphoreType.DMA((2,))],
        ),
        out_shape=[shape((group, n), kind) for n, kind in widths],
        input_output_aliases=aliases,
        compiler_params=params(60),
        cost_estimate=cost(2 * steps * rows * D * (units + wide), 2 * D * (units + wide)),
        name="enter",
    )(*args)


def masked(scores, at, cases, width, begin):
    key_at = lax.broadcasted_iota(jnp.int32, (width, width), 0)
    query_at = lax.broadcasted_iota(jnp.int32, (width, width), 1)
    ok = key_at <= query_at
    if at == cases - 1:
        ok = ok & (key_at + at * width >= begin)
    return jnp.where(ok, scores, -jnp.inf)


def fwd_case(at, cases, width, q_ref, k_ref, v_ref, begin_ref, o_ref, lse_ref):
    first = at * width
    query, begin = q_ref[...], begin_ref[...]
    near = masked(mm(k_ref[first : first + width, :], query, NT), at, cases, width, begin)
    top = jnp.max(near, axis=0, keepdims=True)
    if at:
        far = mm(k_ref[0:first, :], query, NT)
        if at == cases - 1:
            far = far + jnp.where(begin > 0, -jnp.inf, 0.0)
        top = jnp.maximum(top, jnp.max(far, axis=0, keepdims=True))
    near = jnp.exp2((near - top) * SCALE_TWO)
    total = jnp.sum(near, axis=0, keepdims=True)
    if at:
        far = jnp.exp2((far - top) * SCALE_TWO)
        total = total + jnp.sum(far, axis=0, keepdims=True)
    part = 1.0 / total
    out = mm(v_ref[first : first + width, :], (near * part).astype(BF16), TN)
    if at:
        out = out + mm(v_ref[0:first, :], (far * part).astype(BF16), TN)
    o_ref[...] = out.T.astype(BF16)
    lse_ref[0] = top * SCALE_TWO + jnp.log2(total)


def attn_fwd_kernel(cases, width, q_ref, k_ref, v_ref, begin_ref, *rest):
    o_ref, lse_ref = rest[-2:]
    for at in range(cases):

        @pl.when(pl.program_id(1) == at)
        def _(at=at):
            fwd_case(at, cases, width, q_ref, k_ref, v_ref, begin_ref, o_ref, lse_ref)


def attn_fwd(first, count, qkv, begin, old):
    group = qkv.shape[0]
    heads = qkv.shape[1] // (3 * HD)
    width = min(1024, group)
    cases = group // width
    flops = 2 * 2 * count * group * group * HD * 5 // 8
    in_specs = [
        pl.BlockSpec((width, HD), lambda h, i: (i, 3 * (first + h))),
        pl.BlockSpec((group, HD), lambda h, i: (0, 3 * (first + h) + 1)),
        pl.BlockSpec((group, HD), lambda h, i: (0, 3 * (first + h) + 2)),
        pl.BlockSpec((1, width), lambda h, i: (0, i)),
    ]
    args, aliases = [qkv, qkv, qkv, begin], {}
    if old is not None:
        aliases = {len(args) + i: i for i in range(2)}
        in_specs += [HBM] * 2
        args += list(old)
    return pl.pallas_call(
        functools.partial(attn_fwd_kernel, cases, width),
        grid=(count, cases),
        in_specs=in_specs,
        out_specs=[
            pl.BlockSpec((width, HD), lambda h, i: (i, first + h)),
            pl.BlockSpec((1, 1, width), lambda h, i: (first + h, 0, i)),
        ],
        out_shape=[shape((group, heads * HD), BF16), shape((heads, 1, group), F32)],
        input_output_aliases=aliases,
        compiler_params=params(56),
        cost_estimate=cost(4 * flops, 8 * group * count * HD, count * group * group * 5 // 8),
        name="attend",
    )(*args)


def bwd_case(at, cases, width, refs):
    (q_ref, k_ref, v_ref, do_ref, begin_ref, lse_ref, dk_acc, dv_acc) = refs
    first = at * width
    query, dctx, begin, lse = q_ref[...], do_ref[...], begin_ref[...], lse_ref[0]
    spans = [slice(first, first + width)] + ([slice(0, first)] if at else [])
    parts = []
    for span in spans:
        scores = mm(k_ref[span, :], query, NT) * SCALE_TWO - lse
        if span.start == first:
            scores = masked(scores, at, cases, width, begin)
        elif at == cases - 1:
            scores = scores + jnp.where(begin > 0, -jnp.inf, 0.0)
        prob = jnp.exp2(scores)
        dprob = mm(v_ref[span, :], dctx, NT)
        parts.append((span, prob, dprob, jnp.sum(prob * dprob, axis=0, keepdims=True)))
    inner = sum(p[3] for p in parts)
    dq = None
    for span, prob, dprob, _ in parts:
        dscores = (prob * (dprob - inner)).astype(BF16)
        dv_acc[span, :] += mm(prob.astype(BF16), dctx)
        dk_acc[span, :] += mm(dscores, query)
        more = mm(k_ref[span, :], dscores, TN)
        dq = more if dq is None else dq + more
    return dq.T


def attn_bwd_kernel(
    cases, width, q_ref, k_ref, v_ref, do_ref, begin_ref, lse_ref, cos_ref, low_ref, high_ref,
    out_ref, sum_ref, dk_acc, dv_acc,
):
    step = pl.program_id(1)

    @pl.when(step == 0)
    def _():
        dk_acc[...] = jnp.zeros_like(dk_acc)
        dv_acc[...] = jnp.zeros_like(dv_acc)

    refs = (q_ref, k_ref, v_ref, do_ref, begin_ref, lse_ref, dk_acc, dv_acc)
    for at in range(cases):

        @pl.when(step == at)
        def _(at=at):
            dq = bwd_case(at, cases, width, refs) * (HD**-0.5)
            span = slice(at * width, (at + 1) * width)
            back = turn_back(dq, cos_ref[span, :], low_ref[span, :], high_ref[span, :])
            out_ref[span, 0:HD] = back.astype(BF16)

    @pl.when(step == cases - 1)
    def _():
        dk = dk_acc[...] * (HD**-0.5)
        back = turn_back(dk, cos_ref[...], low_ref[...], high_ref[...])
        out_ref[:, HD : 2 * HD] = back.astype(BF16)
        out_ref[:, 2 * HD : 3 * HD] = dv_acc[...].astype(BF16)
        total = jnp.sum(out_ref[...].astype(F32), axis=0, keepdims=True)
        sum_ref[...] = jnp.broadcast_to(total, sum_ref.shape)


def attn_bwd(qkv, dctx, begin, lse, tables):
    group = qkv.shape[0]
    heads = qkv.shape[1] // (3 * HD)
    width = min(512, group)
    cases = group // width
    table = pl.BlockSpec((group, HD), lambda h, i: (0, 0))
    flops = 5 * 2 * heads * group * group * HD * 5 // 8
    return pl.pallas_call(
        functools.partial(attn_bwd_kernel, cases, width),
        grid=(heads, cases),
        in_specs=[
            pl.BlockSpec((width, HD), lambda h, i: (i, 3 * h)),
            pl.BlockSpec((group, HD), lambda h, i: (0, 3 * h + 1)),
            pl.BlockSpec((group, HD), lambda h, i: (0, 3 * h + 2)),
            pl.BlockSpec((width, HD), lambda h, i: (i, h)),
            pl.BlockSpec((1, width), lambda h, i: (0, i)),
            pl.BlockSpec((1, 1, width), lambda h, i: (h, 0, i)),
            table,
            table,
            table,
        ],
        out_specs=[
            pl.BlockSpec((group, 3 * HD), lambda h, i: (0, h)),
            pl.BlockSpec((8, 3 * HD), lambda h, i: (0, h)),
        ],
        out_shape=[shape((group, heads * 3 * HD), BF16), shape((8, heads * 3 * HD), F32)],
        scratch_shapes=[pltpu.VMEM((group, HD), F32), pltpu.VMEM((group, HD), F32)],
        compiler_params=params(56),
        cost_estimate=cost(flops / 100, 0),
        name="attend_back",
    )(qkv, qkv, qkv, dctx, begin, lse, *tables)


def branch_kernel(units, o_ref, act_ref, w_ref, out_ref):
    total = mm(act_ref[...], w_ref[0:units, :]) + mm(o_ref[...], w_ref[units:, :])
    out_ref[...] = total.astype(BF16)


def branch_all(o, act, w_back):
    group, heads, units = o.shape[0], o.shape[1], act.shape[1]
    rows, tile = 512, D // 2
    return pl.pallas_call(
        functools.partial(branch_kernel, units),
        grid=(D // tile, group // rows),
        in_specs=[
            pl.BlockSpec((rows, heads), lambda j, i: (i, 0)),
            pl.BlockSpec((rows, units), lambda j, i: (i, 0)),
            pl.BlockSpec((heads + units, tile), lambda j, i: (0, j)),
        ],
        out_specs=pl.BlockSpec((rows, tile), lambda j, i: (i, j)),
        out_shape=shape((group, D), BF16),
        compiler_params=params(56),
        cost_estimate=cost(2 * group * D * (heads + units), 2 * D * (heads + units)),
        name="branch",
    )(o, act, w_back)


def leave_kernel(many, units, table, *refs):
    sources, (w_ref, gp_ref) = refs[:many], refs[many : many + 2]
    eo_ref, dh_ref, do_ref, sum_ref, buf, sem = refs[-6:]
    slot = fetch(table, sources, buf, sem)

    @pl.when(pl.program_id(0) == 0)
    def _():
        sum_ref[...] = jnp.zeros_like(sum_ref)

    back = buf[slot]
    eo_ref[...] = back
    tile = min(1024, units)
    for at in range(0, units, tile):
        span = slice(at, at + tile)
        dact = mm(back, w_ref[span, :], NT)
        dhid = (dact * gp_ref[:, span].astype(F32)).astype(BF16)
        dh_ref[:, span] = dhid
        total = jnp.sum(dhid.astype(F32), axis=0, keepdims=True)
        sum_ref[:, span] += jnp.broadcast_to(total, (8, tile))
    do_ref[...] = mm(back, w_ref[units:, :], NT).astype(BF16)


def leave(rows, table, sources, w_back, gp, old):
    many, steps = len(sources), table.shape[0]
    group, units = gp.shape
    heads = w_back.shape[0] - units
    row = lambda n: pl.BlockSpec((rows, n), lambda i, p: (p[i, 0], 0))
    in_specs = [HBM] * many + [
        pl.BlockSpec(w_back.shape, lambda i, p: (0, 0), pipeline_mode=pl.Buffered(1)),
        row(units),
    ]
    args = [table, *sources, w_back, gp]
    aliases = {}
    if old is not None:
        aliases = {len(args) + i: i for i in range(3)}
        in_specs += [HBM] * 3
        args += list(old)
    return pl.pallas_call(
        functools.partial(leave_kernel, many, units),
        grid_spec=pltpu.PrefetchScalarGridSpec(
            num_scalar_prefetch=1,
            grid=(steps,),
            in_specs=in_specs,
            out_specs=[row(D), row(units), row(heads), pl.BlockSpec((8, units), lambda i, p: (0, 0))],
            scratch_shapes=[pltpu.VMEM((2, rows, D), BF16), pltpu.SemaphoreType.DMA((2,))],
        ),
        out_shape=[
            shape((group, D), BF16),
            shape((group, units), BF16),
            shape((group, heads), BF16),
            shape((8, units), F32),
        ],
        input_output_aliases=aliases,
        compiler_params=params(60),
        cost_estimate=cost(2 * steps * rows * D * (units + heads), 2 * D * (units + heads)),
        name="leave",
    )(*args)


def din_kernel(dm_ref, dh_ref, w_ref, x_ref, stat_ref, vec_ref, g_ref, sum_ref):
    units = dh_ref.shape[1]
    left = mm(dm_ref[...], w_ref[:, units:], NT)
    right = mm(dh_ref[...], w_ref[:, 0:units], NT)
    g_ref[...] = (left * vec_ref[0:1, :] + right * vec_ref[2:3, :]).astype(BF16)
    xhat = (x_ref[...].astype(F32) - stat_ref[:, 0:1]) * stat_ref[:, 1:2]
    rows = [left * xhat, left, right * xhat, right]
    sums = jnp.concatenate(
        [jnp.sum(r, axis=0, keepdims=True) for r in rows] + [jnp.zeros((4, left.shape[1]), F32)], axis=0
    )

    @pl.when(pl.program_id(1) == 0)
    def _():
        sum_ref[...] = sums

    @pl.when(pl.program_id(1) > 0)
    def _():
        sum_ref[...] += sums


def din_all(dmixed, dhid, w_in, x, stat, norm_vec):
    group, heads3, units = dmixed.shape[0], dmixed.shape[1], dhid.shape[1]
    rows, tile = 512, 1024
    return pl.pallas_call(
        din_kernel,
        grid=(D // tile, group // rows),
        in_specs=[
            pl.BlockSpec((rows, heads3), lambda j, i: (i, 0)),
            pl.BlockSpec((rows, units), lambda j, i: (i, 0)),
            pl.BlockSpec((tile, heads3 + units), lambda j, i: (j, 0)),
            pl.BlockSpec((rows, tile), lambda j, i: (i, j)),
            pl.BlockSpec((rows, 128), lambda j, i: (i, 0)),
            pl.BlockSpec((6, tile), lambda j, i: (0, j)),
        ],
        out_specs=[
            pl.BlockSpec((rows, tile), lambda j, i: (i, j)),
            pl.BlockSpec((8, tile), lambda j, i: (0, j)),
        ],
        out_shape=[shape((group, D), BF16), shape((8, D), F32)],
        compiler_params=params(60),
        cost_estimate=cost(group * D * (heads3 + units) / 50, 0),
        name="input_back",
    )(dmixed, dhid, w_in, x, stat, norm_vec)


def finish_kernel(place, g_ref, e_ref, x_ref, stat_ref, out_ref):
    grad = g_ref[...].astype(F32)
    rstd = stat_ref[:, 1:2]
    xhat = (x_ref[...].astype(F32) - stat_ref[:, 0:1]) * rstd
    mean = jnp.mean(grad, axis=1, keepdims=True)
    along = jnp.mean(grad * xhat, axis=1, keepdims=True)
    out_ref[...] = (e_ref[...].astype(F32) + rstd * (grad - mean - xhat * along)).astype(BF16)


def finish(place, grad, back, x, stat):
    rows = grad.shape[0]
    tile = min(256, rows)
    steps = rows // tile
    row = pl.BlockSpec((tile, D), lambda i, p: (i, 0))
    return pl.pallas_call(
        finish_kernel,
        grid_spec=pltpu.PrefetchScalarGridSpec(
            num_scalar_prefetch=1,
            grid=(steps,),
            in_specs=[row, row, row, pl.BlockSpec((tile, 128), lambda i, p: (p[0] * steps + i, 0))],
            out_specs=row,
        ),
        out_shape=shape((rows, D), BF16),
        compiler_params=params(32),
        cost_estimate=cost(20 * rows * D, 8 * rows * D),
        name="finish",
    )(place, grad, back, x, stat)


def halves(quads):
    bits = list(range(quads.bit_length() - 1))
    plans = []
    for order in (bits, bits[::-1]):
        first = [i for i in range(quads) if i >> order[0] & 1]
        plans.append((order, first, [i for i in range(quads) if i not in first]))
    return plans


def wgrad_kernel(n_left, n_right, cut_left, quads, place, *refs):
    lefts, rights = refs[:n_left], refs[n_left : n_left + n_right]
    rest = refs[n_left + n_right :]
    pairs = list(zip(lefts, rights)) if cut_left else [(v, rights[0]) for v in lefts]
    pieces, at = [], 0
    for a, b in pairs:
        value = mm(a[...], b[...], TN)
        if cut_left:
            pieces.append(((0, value.shape[0]), slice(at, at + value.shape[1]), value))
            at += value.shape[1]
        else:
            pieces.append(((at, at + value.shape[0]), slice(None), value))
            at += value.shape[0]

    if len(rest) == 1:
        for (low, high), cols, value in pieces:
            rest[0][0, low:high, cols] = value.astype(BF16)
        return
    got, outs = rest[0], rest[1:]
    size = got.shape[1] // 2

    def put(ref, which, half):
        for (low, high), cols, value in pieces:
            start, stop = max(low, half * size), min(high, (half + 1) * size)
            if start < stop:
                part = value[start - low : stop - low] + got[0, start:stop, cols].astype(F32)
                ref[which, start - half * size : stop - half * size, cols] = part.astype(BF16)

    for i in range(quads):

        @pl.when(pl.program_id(0) == i)
        def _(i=i):
            at = 0
            for half, (_, first, others) in enumerate(halves(quads)):
                if i in first:
                    put(outs[at], first.index(i), half)
                else:
                    put(outs[at + 1 + others.index(i)], 0, half)
                at += 1 + len(others)


def wgrad(lefts, rights, cut_left, weight, place, quads, got):
    rows = lefts[0].shape[0]
    whole = lambda n: pl.BlockSpec((rows, n), lambda i, p: (0, 0), pipeline_mode=pl.Buffered(1))
    part = lambda n: pl.BlockSpec((rows, n // (2 * quads)), lambda i, p: (0, 2 * (i ^ p[1]) + p[0]))
    widths = [v.shape[1] for v in lefts], [v.shape[1] for v in rights]
    if cut_left:
        in_specs = [part(n) for n in widths[0]] + [whole(n) for n in widths[1]]
        tile = (widths[0][0] // (2 * quads), sum(widths[1]))
    else:
        in_specs = [whole(n) for n in widths[0]] + [part(n) for n in widths[1]]
        tile = (sum(widths[0]), widths[1][0] // (2 * quads))
    args = [place, *lefts, *rights]
    stacked = pl.BlockSpec((1, *tile), lambda i, p: (i, 0, 0))
    if got is None:
        out_specs, out_shape = [stacked], [shape((quads, *tile), BF16)]
    else:
        in_specs.append(stacked)
        args.append(got)
        out_specs, out_shape = [], []
        for _, first, others in halves(quads):
            for count in [len(first)] + [1] * len(others):
                dims = (count, tile[0] // 2, tile[1])
                out_specs.append(
                    pl.BlockSpec(dims, lambda i, p: (0, 0, 0), pipeline_mode=pl.Buffered(1))
                )
                out_shape.append(shape(dims, BF16))
    flops = rows * tile[0] * tile[1] * 2 * quads * weight
    return pl.pallas_call(
        functools.partial(wgrad_kernel, len(lefts), len(rights), cut_left, quads),
        grid_spec=pltpu.PrefetchScalarGridSpec(
            num_scalar_prefetch=1, grid=(quads,), in_specs=in_specs, out_specs=out_specs
        ),
        out_shape=out_shape,
        compiler_params=params(60),
        cost_estimate=cost(flops, 0),
        name="weight_grad",
    )(*args)


class Spread:
    def __init__(self, outs, quads):
        self.mark, self.quads, self.lanes, self.got, at = outs[0], quads, [], [], 0
        for order, first, others in halves(quads):
            held = {i: [(outs[at + 1 + k], None, 0)] for k, i in enumerate(others)}
            self.lanes.append((order, held))
            self.hand(held, order[0], first, outs[at])
            at += 1 + len(others)

    def hand(self, held, bit, blocks, stack):
        got = lax.ppermute(stack, "quad", [(i, i ^ 1 << bit) for i in range(self.quads)])
        for k, i in enumerate(blocks):
            held[i ^ 1 << bit].append((None, len(self.got), k))
        self.got.append(got)

    def add(self, terms):
        values = [own if at is None else self.got[at][k : k + 1] for own, at, k in terms]
        return sum(v.astype(F32) for v in values)

    def rest(self, *earlier):
        for turn_at in range(1, len(self.lanes[0][0])):
            self.got = after(self.got, *earlier)
            for order, held in self.lanes:
                blocks = [i for i in held if i >> order[turn_at] & 1]
                sums = [self.add(held.pop(i)).astype(BF16) for i in blocks]
                stack = sums[0] if len(sums) == 1 else jnp.concatenate(sums, axis=0)
                self.hand(held, order[turn_at], blocks, stack)
        return self

    def total(self):
        return jnp.concatenate([self.add(held[0])[0] for _, held in self.lanes], axis=0)


def part_kernel(n_left, turns, size, place, *refs):
    lefts, rights, rest = refs[:n_left], refs[n_left : n_left + turns], refs[n_left + turns :]
    base_ref = rest[0] if len(rest) == 4 else None
    out_ref, rows_ref, sem = rest[-3:]

    @pl.when(pl.program_id(0) == 0)
    def _():
        copies, at = [], 0
        for i, left in enumerate(lefts):
            span = slice(at, at + left.shape[1])
            at += left.shape[1]
            for k in range(turns):
                source = left.at[pl.ds(pl.multiple_of(place[2 + k] * size, size), size)]
                target = rows_ref.at[k * size : (k + 1) * size, span]
                copies.append(pltpu.make_async_copy(source, target, sem.at[i, k]))
        for copy in copies:
            copy.start()
        for copy in copies:
            copy.wait()

    right = jnp.concatenate([r[...] for r in rights], axis=0) if turns > 1 else rights[0][...]
    value = mm(rows_ref[...], right, TN)
    if base_ref is not None:
        value = value + base_ref[0]
    out_ref[0] = value.astype(out_ref.dtype)


def wgrad_part(lefts, right, size, place, turns, quads, base):
    widths = [v.shape[1] for v in lefts]
    tile = (sum(widths), right.shape[1] // (2 * quads))
    in_specs = [HBM] * len(lefts) + [
        pl.BlockSpec((size, tile[1]), lambda i, p, k=k: (p[2 + k], 2 * (i ^ p[1]) + p[0]))
        for k in range(turns)
    ]
    args = [place, *lefts] + [right] * turns
    stacked = pl.BlockSpec((1, *tile), lambda i, p: (i, 0, 0))
    if base is not None:
        in_specs.append(stacked)
        args.append(base)
    return pl.pallas_call(
        functools.partial(part_kernel, len(lefts), turns, size),
        grid_spec=pltpu.PrefetchScalarGridSpec(
            num_scalar_prefetch=1,
            grid=(quads,),
            in_specs=in_specs,
            out_specs=stacked,
            scratch_shapes=[
                pltpu.VMEM((turns * size, tile[0]), BF16),
                pltpu.SemaphoreType.DMA((len(lefts), turns)),
            ],
        ),
        out_shape=shape((quads, *tile), F32 if base is None else BF16),
        compiler_params=params(60),
        cost_estimate=cost(size * turns * tile[0] * tile[1] * 2 * quads, 0),
        name="weight_grad_part",
    )(*args)


def line_turns(count):
    table = []
    for place in range(count):
        order = []
        for step in range(1, count):
            if place - step >= 0:
                order.append((True, step))
            if place + step < count:
                order.append((False, step))
        table.append(order)
    return table


def lookup(table, place):
    return jnp.asarray(table, jnp.int32)[place]


class Gather:
    def __init__(self, pieces, count, place):
        self.right, self.left = [[v] for v in pieces], [[v] for v in pieces]
        self.count, self.place = count, place

    def step(self, piece, *earlier):
        count, right, left = self.count, self.right[piece], self.left[piece]
        step = len(right)
        here, there = after((right[-1], left[-1]), *earlier)
        right.append(lax.ppermute(here, "mp", [(i, i + 1) for i in range(step - 1, count - 1)]))
        left.append(lax.ppermute(there, "mp", [(i + 1, i) for i in range(0, count - step)]))

    def last(self):
        return [(r[-1], l[-1]) for r, l in zip(self.right, self.left)]

    def turns(self, first, last, size):
        count, many = self.count, len(self.right)
        each = self.right[0][0].shape[0] // size
        turns = line_turns(count)
        sources, tables = [], [[] for _ in range(count)]
        for turn_at in range(first, last + 1):
            for piece in range(many):
                for i in range(count):
                    side, far = turns[i][turn_at - 1] if turn_at else (True, 0)
                    key = (side, far, piece)
                    if key not in sources:
                        sources.append(key)
                    at = (i - far if side else i + far) * many + piece
                    tables[i] += [[at * each + k, sources.index(key), k] for k in range(each)]
        arrays = [(self.right if side else self.left)[piece][far] for side, far, piece in sources]
        return lookup(tables, self.place), arrays


def everywhere(value, axis, size):
    values = [value] + [
        lax.ppermute(value, axis, [(i, i ^ hop) for i in range(size)]) for hop in range(1, size)
    ]
    while len(values) > 1:
        values = [values[i] + values[i + 1] for i in range(0, len(values), 2)]
    return values[0]


def adam_step(weight, grad, first, second, rate, decay):
    first_new = BETA_ONE * first + (1.0 - BETA_ONE) * grad
    second_new = BETA_TWO * second + (1.0 - BETA_TWO) * grad * grad
    first_hat = first_new / (1.0 - BETA_ONE**STEP)
    second_hat = second_new / (1.0 - BETA_TWO**STEP)
    weight_new = weight - rate * (first_hat / (jnp.sqrt(second_hat) + ADAM_EPS) + decay * weight)
    return (weight_new, first_new, second_new)


def rotation_tables(position):
    half = ROT // 2
    inverse = ROPE_BASE ** (-jnp.arange(half, dtype=F32) * 2.0 / ROT)
    angle = position[:, None] * inverse[None, :]
    cosine, sine = jnp.cos(angle), jnp.sin(angle)
    rows = position.shape[0]
    rest = jnp.zeros((rows, HD - ROT), F32)
    zero = jnp.zeros((rows, half), F32)
    return (
        jnp.concatenate([cosine, cosine, rest + 1.0], axis=1),
        jnp.concatenate([-sine, zero, rest], axis=1),
        jnp.concatenate([zero, sine, rest], axis=1),
    )


def local(
    tokens, cotangent, lengths, w_qkv, w_out, w_up, w_down, norm_vec, b_qkv, b_up,
    m_qkv, m_out, m_up, m_down, m_norm, m_bqkv, m_bup,
    v_qkv, v_out, v_up, v_down, v_norm, v_bqkv, v_bup,
):
    rows = tokens.shape[0]
    count = lax.axis_size("mp")
    quads = lax.axis_size("quad")
    place = lax.axis_index("mp")
    core = lax.axis_index("pair")
    group = rows * count
    dp = ("quad", "pair")

    first_len = lengths[0, 0]
    used = lengths[0, 0] + lengths[0, 1]
    row_ids = jnp.arange(group, dtype=jnp.int32)
    begin = jnp.where(row_ids >= used, used, jnp.where(row_ids >= first_len, first_len, 0))
    begin = begin.astype(jnp.int32)
    tables = rotation_tables((row_ids - begin).astype(F32))
    begin = begin.reshape(1, group)
    own_ids = jnp.arange(rows, dtype=jnp.int32) + place * rows
    live_own = (own_ids < used).astype(BF16)

    sub = min(256, rows)
    back_own = cotangent * live_own[:, None]
    many = rows // sub
    x_line = Gather([tokens[i * sub : (i + 1) * sub] for i in range(many)], count, place)
    for piece in range(many):
        x_line.step(piece)
    full_in = jnp.concatenate([w_up.astype(BF16), w_qkv.astype(BF16)], axis=1)
    full_in = lax.all_gather(full_in, dp, axis=0, tiled=True)
    late_down, late_out = after((w_down, w_out), x_line.last()[0])
    full_back = jnp.concatenate([late_down.astype(BF16), late_out.astype(BF16)], axis=0)
    full_back = lax.all_gather(full_back, dp, axis=1, tiled=True)
    b_up_row, b_qkv_row = b_up.reshape(1, -1), b_qkv.reshape(1, -1)

    for step in range(2, count - 1):
        for piece in range(many):
            x_line.step(piece)
    x_line.step(0)
    enter_rest = (norm_vec, full_in, b_up_row, b_qkv_row, tables)
    table, sources = x_line.turns(0, 1, sub)
    ready = (x_line.right[0][count - 2], x_line.left[0][count - 2])
    state = enter(sub, after(table, ready), sources, *enter_rest, None)
    for piece in range(1, many):
        x_line.step(piece, state[0])
    table, sources = x_line.turns(2, count - 2, sub)
    state = enter(sub, after(table, state[0]), sources, *enter_rest, state)
    e_line = Gather([after(back_own, state[0], x_line.last()[0])], count, place)
    e_line.step(0)
    table, sources = x_line.turns(count - 1, count - 1, sub)
    table = after(table, state[0], x_line.last())
    state = enter(sub, table, sources, *enter_rest, state)
    x_all, a1, a2, stat, act, gelu_slope, qkv = state

    heads = qkv.shape[1] // (3 * HD)
    attended = attn_fwd(0, heads // 2, qkv, begin, None)
    e_line.step(0, attended[0])
    attended, lse = attn_fwd(heads // 2, heads - heads // 2, qkv, begin, attended)
    parts = branch_all(attended, act, full_back)

    def leave_at(first, last, old, *earlier):
        table, sources = e_line.turns(first, last, sub)
        old = None if old is None else old[:3]
        return leave(sub, after(table, *earlier), sources, full_back, gelu_slope, old)

    for step in range(3, count):
        e_line.step(0, parts)
    one = leave_at(0, 1, None, parts)
    two = leave_at(2, count - 2, one, one)
    quad = lax.axis_index("quad")
    here = jnp.stack([core, quad]).astype(jnp.int32)
    there = jnp.stack([1 - core, quad]).astype(jnp.int32)
    arrival = lookup(
        [[i] + [i - far if side else i + far for side, far in line_turns(count)[i]] for i in range(count)],
        place,
    )
    second = (act, attended)
    early = jnp.concatenate([there, arrival[: count - 1]])
    give_second = wgrad_part(second, two[0], rows, after(early, two[1]), count - 1, quads, None)
    three = leave_at(count - 1, count - 1, two, give_second, e_line.last())
    back_rows, dhid, dctx = three[:3]
    grad_bup = (one[3] + two[3] + three[3])[0]
    parts = after(parts, give_second, e_line.last())
    branch = lax.psum_scatter(parts, "mp", scatter_dimension=0, tiled=True)

    def give(product, *earlier):
        half = wgrad(*product, after(there, *earlier), quads, None)[0]
        return lax.ppermute(half, "pair", [(0, 1), (1, 0)]), half

    def settle(product, got, earlier, before_sending):
        return Spread(after(wgrad(*product, after(here, *earlier), quads, got), before_sending), quads)

    late = jnp.concatenate([there, arrival[count - 1 :]])
    mark = wgrad_part(second, back_rows, rows, after(late, dhid), 1, quads, give_second)
    got_second = lax.ppermute(mark, "pair", [(0, 1), (1, 0)])
    got_up, mark = give(((a2,), (dhid,), True, 0.05), mark)
    sum_second = settle((second, (back_rows,), False, 0.05), got_second, (mark,), ())
    dmixed, col_qkv = attn_bwd(qkv, dctx, after(begin, sum_second.mark), lse, tables)
    grad_bqkv = col_qkv[0]
    sum_second.rest(dmixed)
    grad_parts, col = din_all(dmixed, dhid, full_in, x_all, stat, norm_vec)
    grad_rows = lax.psum_scatter(grad_parts, "mp", scatter_dimension=0, tiled=True)
    got_inner, mark = give(((a1,), (dmixed,), True, 16), grad_parts, branch, sum_second.got)
    sum_up = settle(((a2,), (dhid,), True, 0.05), got_up, (mark,), ())
    sum_inner = settle(((a1,), (dmixed,), True, 4), got_inner, (sum_up.mark,), ())
    sum_up.rest(sum_inner.mark)
    sum_inner.rest()
    part_up, part_qkv, sum_second = sum_up.total(), sum_inner.total(), sum_second.total()
    units = act.shape[1]
    part_down, part_out = sum_second[:units], sum_second[units:]
    token_vals = tokens.astype(F32)
    layer_out = (token_vals + branch.astype(F32) + norm_vec[4] + norm_vec[5]).astype(BF16)

    back_vals = back_own.astype(F32)
    out_bias = jnp.sum(back_vals, axis=0)
    small = jnp.concatenate([col[0:4], out_bias[None], out_bias[None]], axis=0)
    local_squares = (
        jnp.sum(part_qkv * part_qkv)
        + jnp.sum(part_out * part_out)
        + jnp.sum(part_up * part_up)
        + jnp.sum(part_down * part_down)
    )
    squares = jnp.broadcast_to(local_squares, (128,))
    packed = jnp.concatenate([grad_bqkv, grad_bup, small.reshape(-1), squares]).reshape(-1, 128)
    packed = everywhere(everywhere(packed, "pair", 2), "quad", quads)
    n_qkv, n_up = grad_bqkv.size // 128, grad_bup.size // 128
    biases, rest = packed[: n_qkv + n_up], packed[n_qkv + n_up :]
    sum_bqkv, sum_bup = biases[:n_qkv].reshape(-1), biases[n_qkv:].reshape(-1)
    rest = rest + jnp.concatenate(
        [jnp.zeros((rest.shape[0] - 1, 128), F32), jnp.full((1, 128), jnp.sum(biases * biases))], axis=0
    )
    rest = everywhere(rest, "mp", count)
    grad_small = rest[:-1].reshape(6, D)
    total_squares = rest[-1, 0]
    grad_in = finish(place.reshape(1).astype(jnp.int32), grad_rows, back_own, tokens, stat)

    grad_norm = jnp.sqrt(total_squares + jnp.sum(grad_small * grad_small))
    factor = jnp.minimum(1.0, CLIP_NORM / (grad_norm + 1e-06))
    rate_big = 2.5 * D ** (-0.5)
    rate_out = 2.5 * max(16 * D // GROUP_TOK, 1) ** (-0.5)
    upd_qkv, mom_qkv, sec_qkv = adam_step(w_qkv, factor * part_qkv, m_qkv, v_qkv, rate_big, DECAY)
    upd_out, mom_out, sec_out = adam_step(w_out, factor * part_out, m_out, v_out, rate_out, DECAY)
    upd_up, mom_up, sec_up = adam_step(w_up, factor * part_up, m_up, v_up, rate_big, DECAY)
    upd_down, mom_down, sec_down = adam_step(
        w_down, factor * part_down, m_down, v_down, rate_big, DECAY
    )
    upd_norm, mom_norm, sec_norm = adam_step(
        norm_vec, factor * grad_small, m_norm, v_norm, RATE_SMALL, 0.0
    )
    upd_bqkv, mom_bqkv, sec_bqkv = adam_step(
        b_qkv, factor * sum_bqkv, m_bqkv, v_bqkv, RATE_SMALL, 0.0
    )
    upd_bup, mom_bup, sec_bup = adam_step(b_up, factor * sum_bup, m_bup, v_bup, RATE_SMALL, 0.0)
    return (
        layer_out, grad_in, grad_norm,
        upd_qkv, upd_out, upd_up, upd_down, upd_norm, upd_bqkv, upd_bup,
        mom_qkv, mom_out, mom_up, mom_down, mom_norm, mom_bqkv, mom_bup,
        sec_qkv, sec_out, sec_up, sec_down, sec_norm, sec_bqkv, sec_bup,
    )


def solution(mesh):
    devices = mesh.devices
    split = Mesh(
        devices.reshape(devices.shape[0] // 2, 2, devices.shape[1]), ("quad", "pair", "mp")
    )
    dp = ("quad", "pair")
    tok, row, col = P(("quad", "pair", "mp"), None), P(dp, "mp"), P("mp", dp)
    weights = (row, col, row, col, P(), P("mp"), P("mp"))
    return jax.shard_map(
        local,
        mesh=split,
        in_specs=(tok, tok, P(dp, None)) + weights * 3,
        out_specs=(tok, tok, P()) + weights * 3,
        check_vma=False,
    )
```

```python
import functools

import jax
import jax.numpy as jnp
from jax import lax
from jax.experimental import pallas as pl
from jax.experimental.pallas import tpu as pltpu
from jax.sharding import Mesh
from jax.sharding import PartitionSpec as P

D = 2048
HD = 128
ROT = 32
GROUP_TOK = 2048
STEP = 10

LN_EPS = 1e-05
ROPE_BASE = 10000.0
CLIP_NORM = 1.0
BETA_ONE = 0.9
BETA_TWO = 0.95
ADAM_EPS = 1e-08
DECAY = 0.01
RATE_SMALL = 1.0

F32 = jnp.float32
BF16 = jnp.bfloat16
MB = 1 << 20
SQRT_HALF = 0.7071067811865476
DENSITY = 0.3989422804014327
SCALE_TWO = HD**-0.5 * 1.4426950408889634

NN = (((1,), (0,)), ((), ()))
NT = (((1,), (1,)), ((), ()))
TN = (((0,), (0,)), ((), ()))


def mm(a, b, dims=NN):
    return lax.dot_general(a, b, dims, preferred_element_type=F32)


def cost(flops, nbytes, trans=0):
    return pl.CostEstimate(flops=int(flops), bytes_accessed=int(nbytes), transcendentals=int(trans))


def params(mib, *sem):
    return pltpu.CompilerParams(
        vmem_limit_bytes=mib * MB, dimension_semantics=sem if sem else None
    )


def shape(dims, dtype):
    return jax.ShapeDtypeStruct(dims, dtype)


HBM = pl.BlockSpec(memory_space=pl.ANY)


def after(value, *earlier):
    return lax.optimization_barrier((value, earlier))[0]


def fetch(table, sources, buf, sem):
    step, last = pl.program_id(0), pl.num_programs(0) - 1
    size = buf.shape[1]

    def start(at):
        slot = lax.rem(at, 2)
        for i, source in enumerate(sources):

            @pl.when(table[at, 1] == i)
            def _(source=source):
                span = pl.ds(pl.multiple_of(table[at, 2] * size, size), size)
                pltpu.make_async_copy(source.at[span], buf.at[slot], sem.at[slot]).start()

    @pl.when(step == 0)
    def _():
        start(step)

    @pl.when(step < last)
    def _():
        start(step + 1)

    slot = lax.rem(step, 2)
    pltpu.make_async_copy(sources[0].at[pl.ds(0, size)], buf.at[slot], sem.at[slot]).wait()
    return slot


def turn(u, cosine, low, high):
    return u * cosine + pltpu.roll(u, HD - ROT // 2, 1) * low + pltpu.roll(u, ROT // 2, 1) * high


def turn_back(g, cosine, low, high):
    return g * cosine - pltpu.roll(g, HD - ROT // 2, 1) * low - pltpu.roll(g, ROT // 2, 1) * high


def enter_kernel(many, units, table, *refs):
    sources = refs[:many]
    vec_ref, w_ref, bu_ref, bq_ref, cos_ref, low_ref, high_ref = refs[many : many + 7]
    xo_ref, a1_ref, a2_ref, stat_ref, act_ref, gp_ref, qkv_ref, buf, sem = refs[-9:]
    slot = fetch(table, sources, buf, sem)
    x_in = buf[slot]
    xo_ref[...] = x_in
    x = x_in.astype(F32)
    mean = jnp.mean(x, axis=1, keepdims=True)
    centre = x - mean
    rstd = lax.rsqrt(jnp.mean(centre * centre, axis=1, keepdims=True) + LN_EPS)
    xhat = centre * rstd
    a1_ref[...] = (xhat * vec_ref[0:1, :] + vec_ref[1:2, :]).astype(BF16)
    a2_ref[...] = (xhat * vec_ref[2:3, :] + vec_ref[3:4, :]).astype(BF16)
    lane = lax.broadcasted_iota(jnp.int32, stat_ref.shape, 1)
    stat_ref[...] = jnp.where(lane == 0, mean, rstd)
    tile = min(1024, units)
    for at in range(0, units, tile):
        span = slice(at, at + tile)
        hidden = mm(a2_ref[...], w_ref[:, span]) + bu_ref[:, span]
        phi_cum = 0.5 + 0.5 * lax.erf(hidden * SQRT_HALF)
        act_ref[:, span] = (hidden * phi_cum).astype(BF16)
        dens = jnp.exp(-0.5 * hidden * hidden) * DENSITY
        gp_ref[:, span] = (phi_cum + hidden * dens).astype(BF16)
    mixed = mm(a1_ref[...], w_ref[:, units:]) + bq_ref[...]
    rotation = (cos_ref[...], low_ref[...], high_ref[...])
    for part in range(mixed.shape[1] // HD):
        piece = mixed[:, part * HD : (part + 1) * HD]
        if part % 3 < 2:
            piece = turn(piece, *rotation)
        qkv_ref[:, part * HD : (part + 1) * HD] = piece.astype(BF16)


def enter(rows, table, sources, norm_vec, w_in, b_up, b_qkv, rotation, old):
    many, steps = len(sources), table.shape[0]
    units, wide = b_up.shape[1], b_qkv.shape[1]
    group = rotation[0].shape[0]
    row = lambda n: pl.BlockSpec((rows, n), lambda i, p: (p[i, 0], 0))
    fixed = lambda v: pl.BlockSpec(v.shape, lambda i, p: (0, 0), pipeline_mode=pl.Buffered(1))
    in_specs = [HBM] * many + [fixed(v) for v in (norm_vec, w_in, b_up, b_qkv)] + [row(HD)] * 3
    args = [table, *sources, norm_vec, w_in, b_up, b_qkv, *rotation]
    widths = ((D, BF16), (D, BF16), (D, BF16), (128, F32), (units, BF16), (units, BF16), (wide, BF16))
    aliases = {}
    if old is not None:
        aliases = {len(args) + i: i for i in range(7)}
        in_specs += [HBM] * 7
        args += list(old)
    return pl.pallas_call(
        functools.partial(enter_kernel, many, units),
        grid_spec=pltpu.PrefetchScalarGridSpec(
            num_scalar_prefetch=1,
            grid=(steps,),
            in_specs=in_specs,
            out_specs=[row(n) for n, _ in widths],
            scratch_shapes=[pltpu.VMEM((2, rows, D), BF16), pltpu.SemaphoreType.DMA((2,))],
        ),
        out_shape=[shape((group, n), kind) for n, kind in widths],
        input_output_aliases=aliases,
        compiler_params=params(60),
        cost_estimate=cost(2 * steps * rows * D * (units + wide), 2 * D * (units + wide)),
        name="enter",
    )(*args)


def masked(scores, at, cases, width, begin):
    key_at = lax.broadcasted_iota(jnp.int32, (width, width), 0)
    query_at = lax.broadcasted_iota(jnp.int32, (width, width), 1)
    ok = key_at <= query_at
    if at == cases - 1:
        ok = ok & (key_at + at * width >= begin)
    return jnp.where(ok, scores, -jnp.inf)


def fwd_case(at, cases, width, q_ref, k_ref, v_ref, begin_ref, o_ref, lse_ref):
    first = at * width
    query, begin = q_ref[...], begin_ref[...]
    near = masked(mm(k_ref[first : first + width, :], query, NT), at, cases, width, begin)
    top = jnp.max(near, axis=0, keepdims=True)
    if at:
        far = mm(k_ref[0:first, :], query, NT)
        if at == cases - 1:
            far = far + jnp.where(begin > 0, -jnp.inf, 0.0)
        top = jnp.maximum(top, jnp.max(far, axis=0, keepdims=True))
    near = jnp.exp2((near - top) * SCALE_TWO)
    total = jnp.sum(near, axis=0, keepdims=True)
    if at:
        far = jnp.exp2((far - top) * SCALE_TWO)
        total = total + jnp.sum(far, axis=0, keepdims=True)
    part = 1.0 / total
    out = mm(v_ref[first : first + width, :], (near * part).astype(BF16), TN)
    if at:
        out = out + mm(v_ref[0:first, :], (far * part).astype(BF16), TN)
    o_ref[...] = out.T.astype(BF16)
    lse_ref[0] = top * SCALE_TWO + jnp.log2(total)


def attn_fwd_kernel(cases, width, q_ref, k_ref, v_ref, begin_ref, *rest):
    o_ref, lse_ref = rest[-2:]
    for at in range(cases):

        @pl.when(pl.program_id(1) == at)
        def _(at=at):
            fwd_case(at, cases, width, q_ref, k_ref, v_ref, begin_ref, o_ref, lse_ref)


def attn_fwd(first, count, qkv, begin, old):
    group = qkv.shape[0]
    heads = qkv.shape[1] // (3 * HD)
    width = min(1024, group)
    cases = group // width
    flops = 2 * 2 * count * group * group * HD * 5 // 8
    in_specs = [
        pl.BlockSpec((width, HD), lambda h, i: (i, 3 * (first + h))),
        pl.BlockSpec((group, HD), lambda h, i: (0, 3 * (first + h) + 1)),
        pl.BlockSpec((group, HD), lambda h, i: (0, 3 * (first + h) + 2)),
        pl.BlockSpec((1, width), lambda h, i: (0, i)),
    ]
    args, aliases = [qkv, qkv, qkv, begin], {}
    if old is not None:
        aliases = {len(args) + i: i for i in range(2)}
        in_specs += [HBM] * 2
        args += list(old)
    return pl.pallas_call(
        functools.partial(attn_fwd_kernel, cases, width),
        grid=(count, cases),
        in_specs=in_specs,
        out_specs=[
            pl.BlockSpec((width, HD), lambda h, i: (i, first + h)),
            pl.BlockSpec((1, 1, width), lambda h, i: (first + h, 0, i)),
        ],
        out_shape=[shape((group, heads * HD), BF16), shape((heads, 1, group), F32)],
        input_output_aliases=aliases,
        compiler_params=params(56),
        cost_estimate=cost(4 * flops, 8 * group * count * HD, count * group * group * 5 // 8),
        name="attend",
    )(*args)


def bwd_case(at, cases, width, refs):
    (q_ref, k_ref, v_ref, do_ref, begin_ref, lse_ref, dk_acc, dv_acc) = refs
    first = at * width
    query, dctx, begin, lse = q_ref[...], do_ref[...], begin_ref[...], lse_ref[0]
    spans = [slice(first, first + width)] + ([slice(0, first)] if at else [])
    parts = []
    for span in spans:
        scores = mm(k_ref[span, :], query, NT) * SCALE_TWO - lse
        if span.start == first:
            scores = masked(scores, at, cases, width, begin)
        elif at == cases - 1:
            scores = scores + jnp.where(begin > 0, -jnp.inf, 0.0)
        prob = jnp.exp2(scores)
        dprob = mm(v_ref[span, :], dctx, NT)
        parts.append((span, prob, dprob, jnp.sum(prob * dprob, axis=0, keepdims=True)))
    inner = sum(p[3] for p in parts)
    dq = None
    for span, prob, dprob, _ in parts:
        dscores = (prob * (dprob - inner)).astype(BF16)
        dv_acc[span, :] += mm(prob.astype(BF16), dctx)
        dk_acc[span, :] += mm(dscores, query)
        more = mm(k_ref[span, :], dscores, TN)
        dq = more if dq is None else dq + more
    return dq.T


def attn_bwd_kernel(
    cases, width, q_ref, k_ref, v_ref, do_ref, begin_ref, lse_ref, cos_ref, low_ref, high_ref,
    out_ref, sum_ref, dk_acc, dv_acc,
):
    step = pl.program_id(1)

    @pl.when(step == 0)
    def _():
        dk_acc[...] = jnp.zeros_like(dk_acc)
        dv_acc[...] = jnp.zeros_like(dv_acc)

    refs = (q_ref, k_ref, v_ref, do_ref, begin_ref, lse_ref, dk_acc, dv_acc)
    for at in range(cases):

        @pl.when(step == at)
        def _(at=at):
            dq = bwd_case(at, cases, width, refs) * (HD**-0.5)
            span = slice(at * width, (at + 1) * width)
            back = turn_back(dq, cos_ref[span, :], low_ref[span, :], high_ref[span, :])
            out_ref[span, 0:HD] = back.astype(BF16)

    @pl.when(step == cases - 1)
    def _():
        dk = dk_acc[...] * (HD**-0.5)
        back = turn_back(dk, cos_ref[...], low_ref[...], high_ref[...])
        out_ref[:, HD : 2 * HD] = back.astype(BF16)
        out_ref[:, 2 * HD : 3 * HD] = dv_acc[...].astype(BF16)
        total = jnp.sum(out_ref[...].astype(F32), axis=0, keepdims=True)
        sum_ref[...] = jnp.broadcast_to(total, sum_ref.shape)


def attn_bwd(qkv, dctx, begin, lse, tables):
    group = qkv.shape[0]
    heads = qkv.shape[1] // (3 * HD)
    width = min(512, group)
    cases = group // width
    table = pl.BlockSpec((group, HD), lambda h, i: (0, 0))
    flops = 5 * 2 * heads * group * group * HD * 5 // 8
    return pl.pallas_call(
        functools.partial(attn_bwd_kernel, cases, width),
        grid=(heads, cases),
        in_specs=[
            pl.BlockSpec((width, HD), lambda h, i: (i, 3 * h)),
            pl.BlockSpec((group, HD), lambda h, i: (0, 3 * h + 1)),
            pl.BlockSpec((group, HD), lambda h, i: (0, 3 * h + 2)),
            pl.BlockSpec((width, HD), lambda h, i: (i, h)),
            pl.BlockSpec((1, width), lambda h, i: (0, i)),
            pl.BlockSpec((1, 1, width), lambda h, i: (h, 0, i)),
            table,
            table,
            table,
        ],
        out_specs=[
            pl.BlockSpec((group, 3 * HD), lambda h, i: (0, h)),
            pl.BlockSpec((8, 3 * HD), lambda h, i: (0, h)),
        ],
        out_shape=[shape((group, heads * 3 * HD), BF16), shape((8, heads * 3 * HD), F32)],
        scratch_shapes=[pltpu.VMEM((group, HD), F32), pltpu.VMEM((group, HD), F32)],
        compiler_params=params(56),
        cost_estimate=cost(flops / 100, 0),
        name="attend_back",
    )(qkv, qkv, qkv, dctx, begin, lse, *tables)


def branch_kernel(units, o_ref, act_ref, w_ref, out_ref):
    total = mm(act_ref[...], w_ref[0:units, :]) + mm(o_ref[...], w_ref[units:, :])
    out_ref[...] = total.astype(BF16)


def branch_all(o, act, w_back):
    group, heads, units = o.shape[0], o.shape[1], act.shape[1]
    rows, tile = 512, D // 2
    return pl.pallas_call(
        functools.partial(branch_kernel, units),
        grid=(D // tile, group // rows),
        in_specs=[
            pl.BlockSpec((rows, heads), lambda j, i: (i, 0)),
            pl.BlockSpec((rows, units), lambda j, i: (i, 0)),
            pl.BlockSpec((heads + units, tile), lambda j, i: (0, j)),
        ],
        out_specs=pl.BlockSpec((rows, tile), lambda j, i: (i, j)),
        out_shape=shape((group, D), BF16),
        compiler_params=params(56),
        cost_estimate=cost(2 * group * D * (heads + units), 2 * D * (heads + units)),
        name="branch",
    )(o, act, w_back)


def leave_kernel(many, units, table, *refs):
    sources, (w_ref, gp_ref) = refs[:many], refs[many : many + 2]
    eo_ref, dh_ref, do_ref, sum_ref, buf, sem = refs[-6:]
    slot = fetch(table, sources, buf, sem)

    @pl.when(pl.program_id(0) == 0)
    def _():
        sum_ref[...] = jnp.zeros_like(sum_ref)

    back = buf[slot]
    eo_ref[...] = back
    tile = min(1024, units)
    for at in range(0, units, tile):
        span = slice(at, at + tile)
        dact = mm(back, w_ref[span, :], NT)
        dhid = (dact * gp_ref[:, span].astype(F32)).astype(BF16)
        dh_ref[:, span] = dhid
        total = jnp.sum(dhid.astype(F32), axis=0, keepdims=True)
        sum_ref[:, span] += jnp.broadcast_to(total, (8, tile))
    do_ref[...] = mm(back, w_ref[units:, :], NT).astype(BF16)


def leave(rows, table, sources, w_back, gp, old):
    many, steps = len(sources), table.shape[0]
    group, units = gp.shape
    heads = w_back.shape[0] - units
    row = lambda n: pl.BlockSpec((rows, n), lambda i, p: (p[i, 0], 0))
    in_specs = [HBM] * many + [
        pl.BlockSpec(w_back.shape, lambda i, p: (0, 0), pipeline_mode=pl.Buffered(1)),
        row(units),
    ]
    args = [table, *sources, w_back, gp]
    aliases = {}
    if old is not None:
        aliases = {len(args) + i: i for i in range(3)}
        in_specs += [HBM] * 3
        args += list(old)
    return pl.pallas_call(
        functools.partial(leave_kernel, many, units),
        grid_spec=pltpu.PrefetchScalarGridSpec(
            num_scalar_prefetch=1,
            grid=(steps,),
            in_specs=in_specs,
            out_specs=[row(D), row(units), row(heads), pl.BlockSpec((8, units), lambda i, p: (0, 0))],
            scratch_shapes=[pltpu.VMEM((2, rows, D), BF16), pltpu.SemaphoreType.DMA((2,))],
        ),
        out_shape=[
            shape((group, D), BF16),
            shape((group, units), BF16),
            shape((group, heads), BF16),
            shape((8, units), F32),
        ],
        input_output_aliases=aliases,
        compiler_params=params(60),
        cost_estimate=cost(2 * steps * rows * D * (units + heads), 2 * D * (units + heads)),
        name="leave",
    )(*args)


def din_kernel(dm_ref, dh_ref, w_ref, x_ref, stat_ref, vec_ref, g_ref, sum_ref):
    units = dh_ref.shape[1]
    left = mm(dm_ref[...], w_ref[:, units:], NT)
    right = mm(dh_ref[...], w_ref[:, 0:units], NT)
    g_ref[...] = (left * vec_ref[0:1, :] + right * vec_ref[2:3, :]).astype(BF16)
    xhat = (x_ref[...].astype(F32) - stat_ref[:, 0:1]) * stat_ref[:, 1:2]
    rows = [left * xhat, left, right * xhat, right]
    sums = jnp.concatenate(
        [jnp.sum(r, axis=0, keepdims=True) for r in rows] + [jnp.zeros((4, left.shape[1]), F32)], axis=0
    )

    @pl.when(pl.program_id(1) == 0)
    def _():
        sum_ref[...] = sums

    @pl.when(pl.program_id(1) > 0)
    def _():
        sum_ref[...] += sums


def din_all(dmixed, dhid, w_in, x, stat, norm_vec):
    group, heads3, units = dmixed.shape[0], dmixed.shape[1], dhid.shape[1]
    rows, tile = 512, 1024
    return pl.pallas_call(
        din_kernel,
        grid=(D // tile, group // rows),
        in_specs=[
            pl.BlockSpec((rows, heads3), lambda j, i: (i, 0)),
            pl.BlockSpec((rows, units), lambda j, i: (i, 0)),
            pl.BlockSpec((tile, heads3 + units), lambda j, i: (j, 0)),
            pl.BlockSpec((rows, tile), lambda j, i: (i, j)),
            pl.BlockSpec((rows, 128), lambda j, i: (i, 0)),
            pl.BlockSpec((6, tile), lambda j, i: (0, j)),
        ],
        out_specs=[
            pl.BlockSpec((rows, tile), lambda j, i: (i, j)),
            pl.BlockSpec((8, tile), lambda j, i: (0, j)),
        ],
        out_shape=[shape((group, D), BF16), shape((8, D), F32)],
        compiler_params=params(60),
        cost_estimate=cost(group * D * (heads3 + units) / 50, 0),
        name="input_back",
    )(dmixed, dhid, w_in, x, stat, norm_vec)


def finish_kernel(place, g_ref, e_ref, x_ref, stat_ref, out_ref):
    grad = g_ref[...].astype(F32)
    rstd = stat_ref[:, 1:2]
    xhat = (x_ref[...].astype(F32) - stat_ref[:, 0:1]) * rstd
    mean = jnp.mean(grad, axis=1, keepdims=True)
    along = jnp.mean(grad * xhat, axis=1, keepdims=True)
    out_ref[...] = (e_ref[...].astype(F32) + rstd * (grad - mean - xhat * along)).astype(BF16)


def finish(place, grad, back, x, stat):
    rows = grad.shape[0]
    tile = min(256, rows)
    steps = rows // tile
    row = pl.BlockSpec((tile, D), lambda i, p: (i, 0))
    return pl.pallas_call(
        finish_kernel,
        grid_spec=pltpu.PrefetchScalarGridSpec(
            num_scalar_prefetch=1,
            grid=(steps,),
            in_specs=[row, row, row, pl.BlockSpec((tile, 128), lambda i, p: (p[0] * steps + i, 0))],
            out_specs=row,
        ),
        out_shape=shape((rows, D), BF16),
        compiler_params=params(60),
        cost_estimate=cost(20 * rows * D, 8 * rows * D),
        name="finish",
    )(place, grad, back, x, stat)


def halves(quads):
    bits = list(range(quads.bit_length() - 1))
    plans = []
    for order in (bits, bits[::-1]):
        first = [i for i in range(quads) if i >> order[0] & 1]
        plans.append((order, first, [i for i in range(quads) if i not in first]))
    return plans


def wgrad_kernel(n_left, n_right, cut_left, quads, place, *refs):
    lefts, rights = refs[:n_left], refs[n_left : n_left + n_right]
    rest = refs[n_left + n_right :]
    pairs = list(zip(lefts, rights)) if cut_left else [(v, rights[0]) for v in lefts]
    pieces, at = [], 0
    for a, b in pairs:
        value = mm(a[...], b[...], TN)
        if cut_left:
            pieces.append(((0, value.shape[0]), slice(at, at + value.shape[1]), value))
            at += value.shape[1]
        else:
            pieces.append(((at, at + value.shape[0]), slice(None), value))
            at += value.shape[0]

    if len(rest) == 1:
        for (low, high), cols, value in pieces:
            rest[0][0, low:high, cols] = value.astype(BF16)
        return
    got, outs = rest[0], rest[1:]
    size = got.shape[1] // 2

    def put(ref, which, half):
        for (low, high), cols, value in pieces:
            start, stop = max(low, half * size), min(high, (half + 1) * size)
            if start < stop:
                part = value[start - low : stop - low] + got[0, start:stop, cols].astype(F32)
                ref[which, start - half * size : stop - half * size, cols] = part.astype(BF16)

    for i in range(quads):

        @pl.when(pl.program_id(0) == i)
        def _(i=i):
            at = 0
            for half, (_, first, others) in enumerate(halves(quads)):
                if i in first:
                    put(outs[at], first.index(i), half)
                else:
                    put(outs[at + 1 + others.index(i)], 0, half)
                at += 1 + len(others)


def wgrad(lefts, rights, cut_left, weight, place, quads, got):
    rows = lefts[0].shape[0]
    whole = lambda n: pl.BlockSpec((rows, n), lambda i, p: (0, 0), pipeline_mode=pl.Buffered(1))
    part = lambda n: pl.BlockSpec((rows, n // (2 * quads)), lambda i, p: (0, 2 * (i ^ p[1]) + p[0]))
    widths = [v.shape[1] for v in lefts], [v.shape[1] for v in rights]
    if cut_left:
        in_specs = [part(n) for n in widths[0]] + [whole(n) for n in widths[1]]
        tile = (widths[0][0] // (2 * quads), sum(widths[1]))
    else:
        in_specs = [whole(n) for n in widths[0]] + [part(n) for n in widths[1]]
        tile = (sum(widths[0]), widths[1][0] // (2 * quads))
    args = [place, *lefts, *rights]
    stacked = pl.BlockSpec((1, *tile), lambda i, p: (i, 0, 0))
    if got is None:
        out_specs, out_shape = [stacked], [shape((quads, *tile), BF16)]
    else:
        in_specs.append(stacked)
        args.append(got)
        out_specs, out_shape = [], []
        for _, first, others in halves(quads):
            for count in [len(first)] + [1] * len(others):
                dims = (count, tile[0] // 2, tile[1])
                out_specs.append(
                    pl.BlockSpec(dims, lambda i, p: (0, 0, 0), pipeline_mode=pl.Buffered(1))
                )
                out_shape.append(shape(dims, BF16))
    flops = rows * tile[0] * tile[1] * 2 * quads * weight
    return pl.pallas_call(
        functools.partial(wgrad_kernel, len(lefts), len(rights), cut_left, quads),
        grid_spec=pltpu.PrefetchScalarGridSpec(
            num_scalar_prefetch=1, grid=(quads,), in_specs=in_specs, out_specs=out_specs
        ),
        out_shape=out_shape,
        compiler_params=params(60),
        cost_estimate=cost(flops, 0),
        name="weight_grad",
    )(*args)


class Spread:
    def __init__(self, outs, quads):
        self.mark, self.quads, self.lanes, self.got, at = outs[0], quads, [], [], 0
        for order, first, others in halves(quads):
            held = {i: [(outs[at + 1 + k], None, 0)] for k, i in enumerate(others)}
            self.lanes.append((order, held))
            self.hand(held, order[0], first, outs[at])
            at += 1 + len(others)

    def hand(self, held, bit, blocks, stack):
        got = lax.ppermute(stack, "quad", [(i, i ^ 1 << bit) for i in range(self.quads)])
        for k, i in enumerate(blocks):
            held[i ^ 1 << bit].append((None, len(self.got), k))
        self.got.append(got)

    def add(self, terms):
        values = [own if at is None else self.got[at][k : k + 1] for own, at, k in terms]
        return sum(v.astype(F32) for v in values)

    def rest(self, *earlier):
        for turn_at in range(1, len(self.lanes[0][0])):
            self.got = after(self.got, *earlier)
            for order, held in self.lanes:
                blocks = [i for i in held if i >> order[turn_at] & 1]
                sums = [self.add(held.pop(i)).astype(BF16) for i in blocks]
                stack = sums[0] if len(sums) == 1 else jnp.concatenate(sums, axis=0)
                self.hand(held, order[turn_at], blocks, stack)
        return self

    def total(self):
        return jnp.concatenate([self.add(held[0])[0] for _, held in self.lanes], axis=0)


def part_kernel(n_left, turns, size, place, *refs):
    lefts, rights, rest = refs[:n_left], refs[n_left : n_left + turns], refs[n_left + turns :]
    base_ref = rest[0] if len(rest) == 4 else None
    out_ref, rows_ref, sem = rest[-3:]

    @pl.when(pl.program_id(0) == 0)
    def _():
        copies, at = [], 0
        for i, left in enumerate(lefts):
            span = slice(at, at + left.shape[1])
            at += left.shape[1]
            for k in range(turns):
                source = left.at[pl.ds(pl.multiple_of(place[2 + k] * size, size), size)]
                target = rows_ref.at[k * size : (k + 1) * size, span]
                copies.append(pltpu.make_async_copy(source, target, sem.at[i, k]))
        for copy in copies:
            copy.start()
        for copy in copies:
            copy.wait()

    right = jnp.concatenate([r[...] for r in rights], axis=0) if turns > 1 else rights[0][...]
    value = mm(rows_ref[...], right, TN)
    if base_ref is not None:
        value = value + base_ref[0]
    out_ref[0] = value.astype(out_ref.dtype)


def wgrad_part(lefts, right, size, place, turns, quads, base):
    widths = [v.shape[1] for v in lefts]
    tile = (sum(widths), right.shape[1] // (2 * quads))
    in_specs = [HBM] * len(lefts) + [
        pl.BlockSpec((size, tile[1]), lambda i, p, k=k: (p[2 + k], 2 * (i ^ p[1]) + p[0]))
        for k in range(turns)
    ]
    args = [place, *lefts] + [right] * turns
    stacked = pl.BlockSpec((1, *tile), lambda i, p: (i, 0, 0))
    if base is not None:
        in_specs.append(stacked)
        args.append(base)
    return pl.pallas_call(
        functools.partial(part_kernel, len(lefts), turns, size),
        grid_spec=pltpu.PrefetchScalarGridSpec(
            num_scalar_prefetch=1,
            grid=(quads,),
            in_specs=in_specs,
            out_specs=stacked,
            scratch_shapes=[
                pltpu.VMEM((turns * size, tile[0]), BF16),
                pltpu.SemaphoreType.DMA((len(lefts), turns)),
            ],
        ),
        out_shape=shape((quads, *tile), F32 if base is None else BF16),
        compiler_params=params(60),
        cost_estimate=cost(size * turns * tile[0] * tile[1] * 2 * quads, 0),
        name="weight_grad_part",
    )(*args)


def line_turns(count):
    table = []
    for place in range(count):
        order = []
        for step in range(1, count):
            if place - step >= 0:
                order.append((True, step))
            if place + step < count:
                order.append((False, step))
        table.append(order)
    return table


def lookup(table, place):
    return jnp.asarray(table, jnp.int32)[place]


class Gather:
    def __init__(self, pieces, count, place):
        self.right, self.left = [[v] for v in pieces], [[v] for v in pieces]
        self.count, self.place = count, place

    def step(self, piece, *earlier):
        count, right, left = self.count, self.right[piece], self.left[piece]
        step = len(right)
        here, there = after((right[-1], left[-1]), *earlier)
        right.append(lax.ppermute(here, "mp", [(i, i + 1) for i in range(step - 1, count - 1)]))
        left.append(lax.ppermute(there, "mp", [(i + 1, i) for i in range(0, count - step)]))

    def last(self):
        return [(r[-1], l[-1]) for r, l in zip(self.right, self.left)]

    def turns(self, first, last, size):
        count, many = self.count, len(self.right)
        each = self.right[0][0].shape[0] // size
        turns = line_turns(count)
        sources, tables = [], [[] for _ in range(count)]
        for turn_at in range(first, last + 1):
            for piece in range(many):
                for i in range(count):
                    side, far = turns[i][turn_at - 1] if turn_at else (True, 0)
                    key = (side, far, piece)
                    if key not in sources:
                        sources.append(key)
                    at = (i - far if side else i + far) * many + piece
                    tables[i] += [[at * each + k, sources.index(key), k] for k in range(each)]
        arrays = [(self.right if side else self.left)[piece][far] for side, far, piece in sources]
        return lookup(tables, self.place), arrays


def everywhere(value, axis, size):
    values = [value] + [
        lax.ppermute(value, axis, [(i, i ^ hop) for i in range(size)]) for hop in range(1, size)
    ]
    while len(values) > 1:
        values = [values[i] + values[i + 1] for i in range(0, len(values), 2)]
    return values[0]


def adam_step(weight, grad, first, second, rate, decay):
    first_new = BETA_ONE * first + (1.0 - BETA_ONE) * grad
    second_new = BETA_TWO * second + (1.0 - BETA_TWO) * grad * grad
    first_hat = first_new / (1.0 - BETA_ONE**STEP)
    second_hat = second_new / (1.0 - BETA_TWO**STEP)
    weight_new = weight - rate * (first_hat / (jnp.sqrt(second_hat) + ADAM_EPS) + decay * weight)
    return (weight_new, first_new, second_new)


def adam_kernel(rates, factor_ref, *refs):
    ins, outs = refs[: 4 * len(rates)], refs[4 * len(rates) :]
    factor = factor_ref[0]
    for i, rate in enumerate(rates):
        weight, grad, first, second = (r[...] for r in ins[4 * i : 4 * i + 4])
        for ref, new in zip(outs[3 * i : 3 * i + 3], adam_step(weight, factor * grad, first, second, rate, DECAY)):
            ref[...] = new


def adam_all(factor, groups):
    steps = 8
    in_specs, out_specs, out_shape, args = [], [], [], []
    for weight, grad, low, first, second, _ in groups:
        rows, cols = weight.shape[0] // steps, weight.shape[1]
        spec = pl.BlockSpec((rows, cols), lambda i, p: (i, 0))
        shifted = pl.BlockSpec((rows, cols), lambda i, p, at=low // rows: (at + i, 0))
        in_specs += [spec, shifted, spec, spec]
        args += [weight, grad, first, second]
        out_specs += [spec] * 3
        out_shape += [shape(weight.shape, F32)] * 3
    return pl.pallas_call(
        functools.partial(adam_kernel, [g[-1] for g in groups]),
        grid_spec=pltpu.PrefetchScalarGridSpec(
            num_scalar_prefetch=1, grid=(steps,), in_specs=in_specs, out_specs=out_specs
        ),
        out_shape=out_shape,
        compiler_params=params(60),
        cost_estimate=cost(0, 28 * sum(g[0].size for g in groups)),
        name="adam",
    )(factor, *args)


def rotation_tables(position):
    half = ROT // 2
    inverse = ROPE_BASE ** (-jnp.arange(half, dtype=F32) * 2.0 / ROT)
    angle = position[:, None] * inverse[None, :]
    cosine, sine = jnp.cos(angle), jnp.sin(angle)
    rows = position.shape[0]
    rest = jnp.zeros((rows, HD - ROT), F32)
    zero = jnp.zeros((rows, half), F32)
    return (
        jnp.concatenate([cosine, cosine, rest + 1.0], axis=1),
        jnp.concatenate([-sine, zero, rest], axis=1),
        jnp.concatenate([zero, sine, rest], axis=1),
    )


def local(
    tokens, cotangent, lengths, w_qkv, w_out, w_up, w_down, norm_vec, b_qkv, b_up,
    m_qkv, m_out, m_up, m_down, m_norm, m_bqkv, m_bup,
    v_qkv, v_out, v_up, v_down, v_norm, v_bqkv, v_bup,
):
    rows = tokens.shape[0]
    count = lax.axis_size("mp")
    quads = lax.axis_size("quad")
    place = lax.axis_index("mp")
    core = lax.axis_index("pair")
    group = rows * count
    dp = ("quad", "pair")

    first_len = lengths[0, 0]
    used = lengths[0, 0] + lengths[0, 1]
    row_ids = jnp.arange(group, dtype=jnp.int32)
    begin = jnp.where(row_ids >= used, used, jnp.where(row_ids >= first_len, first_len, 0))
    begin = begin.astype(jnp.int32)
    tables = rotation_tables((row_ids - begin).astype(F32))
    begin = begin.reshape(1, group)
    own_ids = jnp.arange(rows, dtype=jnp.int32) + place * rows
    live_own = (own_ids < used).astype(BF16)

    sub = min(256, rows)
    back_own = cotangent * live_own[:, None]
    many = rows // sub
    x_line = Gather([tokens[i * sub : (i + 1) * sub] for i in range(many)], count, place)
    for piece in range(many):
        x_line.step(piece)
    full_in = jnp.concatenate([w_up.astype(BF16), w_qkv.astype(BF16)], axis=1)
    full_in = lax.all_gather(full_in, dp, axis=0, tiled=True)
    late_down, late_out = after((w_down, w_out), x_line.last()[0])
    full_back = jnp.concatenate([late_down.astype(BF16), late_out.astype(BF16)], axis=0)
    full_back = lax.all_gather(full_back, dp, axis=1, tiled=True)
    b_up_row, b_qkv_row = b_up.reshape(1, -1), b_qkv.reshape(1, -1)

    for step in range(2, count - 1):
        for piece in range(many):
            x_line.step(piece)
    x_line.step(0)
    enter_rest = (norm_vec, full_in, b_up_row, b_qkv_row, tables)
    table, sources = x_line.turns(0, 1, sub)
    ready = (x_line.right[0][count - 2], x_line.left[0][count - 2])
    state = enter(sub, after(table, ready), sources, *enter_rest, None)
    for piece in range(1, many):
        x_line.step(piece, state[0])
    table, sources = x_line.turns(2, count - 2, sub)
    state = enter(sub, after(table, state[0]), sources, *enter_rest, state)
    e_line = Gather([after(back_own, state[0], x_line.last()[0])], count, place)
    e_line.step(0)
    table, sources = x_line.turns(count - 1, count - 1, sub)
    table = after(table, state[0], x_line.last())
    state = enter(sub, table, sources, *enter_rest, state)
    x_all, a1, a2, stat, act, gelu_slope, qkv = state

    heads = qkv.shape[1] // (3 * HD)
    attended = attn_fwd(0, heads // 2, qkv, begin, None)
    e_line.step(0, attended[0])
    attended, lse = attn_fwd(heads // 2, heads - heads // 2, qkv, begin, attended)
    parts = branch_all(attended, act, full_back)

    def leave_at(first, last, old, *earlier):
        table, sources = e_line.turns(first, last, sub)
        old = None if old is None else old[:3]
        return leave(sub, after(table, *earlier), sources, full_back, gelu_slope, old)

    for step in range(3, count):
        e_line.step(0, parts)
    one = leave_at(0, 1, None, parts)
    two = leave_at(2, count - 2, one, one)
    quad = lax.axis_index("quad")
    here = jnp.stack([core, quad]).astype(jnp.int32)
    there = jnp.stack([1 - core, quad]).astype(jnp.int32)
    arrival = lookup(
        [[i] + [i - far if side else i + far for side, far in line_turns(count)[i]] for i in range(count)],
        place,
    )
    second = (act, attended)
    early = jnp.concatenate([there, arrival[: count - 1]])
    give_second = wgrad_part(second, two[0], rows, after(early, two[1]), count - 1, quads, None)
    three = leave_at(count - 1, count - 1, two, give_second, e_line.last())
    back_rows, dhid, dctx = three[:3]
    grad_bup = (one[3] + two[3] + three[3])[0]
    parts = after(parts, give_second, e_line.last())
    branch = lax.psum_scatter(parts, "mp", scatter_dimension=0, tiled=True)

    def give(product, *earlier):
        half = wgrad(*product, after(there, *earlier), quads, None)[0]
        return lax.ppermute(half, "pair", [(0, 1), (1, 0)]), half

    def settle(product, got, earlier, before_sending):
        return Spread(after(wgrad(*product, after(here, *earlier), quads, got), before_sending), quads)

    late = jnp.concatenate([there, arrival[count - 1 :]])
    mark = wgrad_part(second, back_rows, rows, after(late, dhid), 1, quads, give_second)
    got_second = lax.ppermute(mark, "pair", [(0, 1), (1, 0)])
    got_up, mark = give(((a2,), (dhid,), True, 0.05), mark)
    sum_second = settle((second, (back_rows,), False, 0.05), got_second, (mark,), ())
    dmixed, col_qkv = attn_bwd(qkv, dctx, after(begin, sum_second.mark), lse, tables)
    grad_bqkv = col_qkv[0]
    sum_second.rest(dmixed)
    grad_parts, col = din_all(dmixed, dhid, full_in, x_all, stat, norm_vec)
    grad_rows = lax.psum_scatter(grad_parts, "mp", scatter_dimension=0, tiled=True)
    got_inner, mark = give(((a1,), (dmixed,), True, 16), grad_parts, branch, sum_second.got)
    sum_up = settle(((a2,), (dhid,), True, 0.05), got_up, (mark,), ())
    sum_inner = settle(((a1,), (dmixed,), True, 4), got_inner, (sum_up.mark,), ())
    sum_up.rest(sum_inner.mark)
    sum_inner.rest()
    part_up, part_qkv, sum_second = sum_up.total(), sum_inner.total(), sum_second.total()
    units = act.shape[1]
    token_vals = tokens.astype(F32)
    layer_out = (token_vals + branch.astype(F32) + norm_vec[4] + norm_vec[5]).astype(BF16)

    back_vals = back_own.astype(F32)
    out_bias = jnp.sum(back_vals, axis=0)
    small = jnp.concatenate([col[0:4], out_bias[None], out_bias[None]], axis=0)
    local_squares = (
        jnp.sum(part_qkv * part_qkv)
        + jnp.sum(part_up * part_up)
        + jnp.sum(sum_second * sum_second)
    )
    squares = jnp.broadcast_to(local_squares, (128,))
    packed = jnp.concatenate([grad_bqkv, grad_bup, small.reshape(-1), squares]).reshape(-1, 128)
    packed = everywhere(everywhere(packed, "pair", 2), "quad", quads)
    n_qkv, n_up = grad_bqkv.size // 128, grad_bup.size // 128
    biases, rest = packed[: n_qkv + n_up], packed[n_qkv + n_up :]
    sum_bqkv, sum_bup = biases[:n_qkv].reshape(-1), biases[n_qkv:].reshape(-1)
    rest = rest + jnp.concatenate(
        [jnp.zeros((rest.shape[0] - 1, 128), F32), jnp.full((1, 128), jnp.sum(biases * biases))], axis=0
    )
    rest = everywhere(rest, "mp", count)
    grad_small = rest[:-1].reshape(6, D)
    total_squares = rest[-1, 0]
    grad_in = finish(place.reshape(1).astype(jnp.int32), grad_rows, back_own, tokens, stat)

    grad_norm = jnp.sqrt(total_squares + jnp.sum(grad_small * grad_small))
    factor = jnp.minimum(1.0, CLIP_NORM / (grad_norm + 1e-06))
    rate_big = 2.5 * D ** (-0.5)
    rate_out = 2.5 * max(16 * D // GROUP_TOK, 1) ** (-0.5)
    (
        upd_qkv, mom_qkv, sec_qkv, upd_out, mom_out, sec_out,
        upd_up, mom_up, sec_up, upd_down, mom_down, sec_down,
    ) = adam_all(
        factor.reshape(1),
        (
            (w_qkv, part_qkv, 0, m_qkv, v_qkv, rate_big),
            (w_out, sum_second, units, m_out, v_out, rate_out),
            (w_up, part_up, 0, m_up, v_up, rate_big),
            (w_down, sum_second, 0, m_down, v_down, rate_big),
        ),
    )
    upd_norm, mom_norm, sec_norm = adam_step(
        norm_vec, factor * grad_small, m_norm, v_norm, RATE_SMALL, 0.0
    )
    upd_bqkv, mom_bqkv, sec_bqkv = adam_step(
        b_qkv, factor * sum_bqkv, m_bqkv, v_bqkv, RATE_SMALL, 0.0
    )
    upd_bup, mom_bup, sec_bup = adam_step(b_up, factor * sum_bup, m_bup, v_bup, RATE_SMALL, 0.0)
    return (
        layer_out, grad_in, grad_norm,
        upd_qkv, upd_out, upd_up, upd_down, upd_norm, upd_bqkv, upd_bup,
        mom_qkv, mom_out, mom_up, mom_down, mom_norm, mom_bqkv, mom_bup,
        sec_qkv, sec_out, sec_up, sec_down, sec_norm, sec_bqkv, sec_bup,
    )


def solution(mesh):
    devices = mesh.devices
    split = Mesh(
        devices.reshape(devices.shape[0] // 2, 2, devices.shape[1]), ("quad", "pair", "mp")
    )
    dp = ("quad", "pair")
    tok, row, col = P(("quad", "pair", "mp"), None), P(dp, "mp"), P("mp", dp)
    weights = (row, col, row, col, P(), P("mp"), P("mp"))
    return jax.shard_map(
        local,
        mesh=split,
        in_specs=(tok, tok, P(dp, None)) + weights * 3,
        out_specs=(tok, tok, P()) + weights * 3,
        check_vma=False,
    )
```
